32 devices in a mesh: pair: 8 (over z, y), state: 4 (over x, core).
Axes of the slice: x: 2, y: 2, z: 4, core: 2. Of those that a mesh axis runs over, the one named last changes fastest.
Arguments:
- states_in: float32 [64, 53248], P('state', 'pair'), may hold values from -6 to 6
- onsite: float32 [53248], P('pair'), may hold values from -1 to 1
- node_features: bfloat16 [4096, 512], P('pair', 'state'), may hold values from -6 to 6
- atom_orbitals: int32 [4096], replicated, may hold values from 4 to 13
- pair_blocks: int32 [64, 2], replicated, may hold values from 0 to 63, as said below
- pair_live: int32 [64], replicated, may hold values from 0 to 1, as said below
- weight_in: bfloat16 [512, 512], replicated, may hold values from -0.25 to 0.25
- bias_in: float32 [512], replicated, may hold values from -3 to 3
- weight_out: bfloat16 [512, 169], replicated, may hold values from -0.009765625 to 0.009765625
Outputs:
- first_step: float32 [64, 53248], P('state', 'pair')
- second_step: float32 [64, 53248], P('state', 'pair')
The draws below stay inside these ranges and needn't reach their ends.
Inputs may be any that keep to these rules, and one draw needn't show every extreme that they name: `pair_blocks`: pair slot k belongs to index k // 8 of pair, and block b to index b // 8. The two blocks of a pair differ; of the 16 blocks named by the pair slots of one index of pair, live or not, at most 2 lie on any one index, and some index holds 2 of them. `pair_live`: the live slots of each index of pair come first among its 8 slots; every index has at least one, and some index has all 8 live.
All inputs are finite; a program needn't handle non-finite values.
Results may differ from the reference program's by a relative error of at most 0.0034.
Values may be sent and summed in bfloat16 or wider, within the bound.
No kernel may reach another device: no remote copies, remote signals or barrier semaphores. Data moves between devices by JAX's collectives and lax.ppermute only.
A program may use at most 192 MiB of HBM per device.

```python
import jax
import jax.numpy as jnp
from jax import lax

FEAT = 512
HID = 512
ORB = 13
ATOM_BLK = 64
BLK_DEV = 8
PAIR_DEV = 8
OUTW = 169
BO = 832
STATES = 64
NB = 64
ATOMS = 4096
NORB = 53248
PAIRS = 64


def pair_layout(key):
    base_key = jax.random.fold_in(key, 31)
    owner_count = NB // BLK_DEV
    end_count = 2 * PAIR_DEV
    capacity = (end_count + owner_count - 1) // owner_count
    slot_keys = jax.random.split(jax.random.fold_in(base_key, 1), owner_count)
    slot_draws = jax.vmap(lambda one_key: jax.random.permutation(one_key, owner_count * capacity)[:end_count])(slot_keys)
    owners = slot_draws // capacity
    local_index = jax.random.randint(jax.random.fold_in(base_key, 2), (owner_count, end_count), 0, BLK_DEV)
    offset = jax.random.randint(jax.random.fold_in(base_key, 3), (owner_count, PAIR_DEV), 1, BLK_DEV)
    first_owner = owners[:, 0::2]
    second_owner = owners[:, 1::2]
    first_local = local_index[:, 0::2]
    second_local = jnp.where(first_owner == second_owner, (first_local + offset) % BLK_DEV, local_index[:, 1::2])
    first_block = first_owner * BLK_DEV + first_local
    second_block = second_owner * BLK_DEV + second_local
    blocks = jnp.stack([first_block, second_block], axis=-1).reshape(owner_count * PAIR_DEV, 2).astype(jnp.int32)
    first_count = jax.random.randint(jax.random.fold_in(base_key, 4), (owner_count,), 1, PAIR_DEV + 1)
    second_count = jax.random.randint(jax.random.fold_in(base_key, 5), (owner_count,), 1, PAIR_DEV + 1)
    live_count = jnp.minimum(first_count, second_count)
    busiest = jax.random.randint(jax.random.fold_in(base_key, 6), (), 0, owner_count)
    live_count = jnp.where(jnp.arange(owner_count) == busiest, PAIR_DEV, live_count)
    live_mask = (jnp.arange(PAIR_DEV)[None, :] < live_count[:, None]).astype(jnp.int32).reshape(owner_count * PAIR_DEV)
    return (blocks, live_mask)


def draw_pair_blocks(key, part):
    return pair_layout(key)[0]


def draw_pair_live(key, part):
    return pair_layout(key)[1]


def touch_ends(drawn, own_key, low, largest):
    longest = drawn.shape.index(max(drawn.shape))
    spots = []
    for shift in (0, 1):
        where = [jax.random.randint(jax.random.fold_in(own_key, axis), (), 0, length) for axis, length in enumerate(drawn.shape)]
        where[longest] = (where[longest] + shift) % drawn.shape[longest]
        spots.append(tuple(where))
    return drawn.at[spots[0]].set(low).at[spots[1]].set(largest)


def levels(stream_key, extent, cuts, smallest, high):
    gain, own = 1.0, jax.random.fold_in(stream_key, 6)
    for dim, blocks in cuts:
        draws = jnp.exp(jax.random.uniform(jax.random.fold_in(own, dim), (blocks,), jnp.float32, smallest / len(cuts), high / len(cuts)))
        gain = gain * jnp.repeat(draws, extent[dim] // blocks).reshape([-1 if axis == dim else 1 for axis in range(len(extent))])
    return gain


def bell_draw(key, extent, spread, most, cuts=(), held_as=jnp.bfloat16):
    result = jax.random.normal(key, extent, jnp.float32) * spread
    if len(cuts) > 0:
        result = levels(key, extent, cuts, -0.22, 0.18) * result
    return jnp.clip(result, min=-most, max=most).astype(held_as)


def setup_inputs(seed: int = 0) -> dict:
    key_of = jax.random.split(jax.random.key(seed), 10)
    states_in = bell_draw(key_of[0], (STATES, NORB), 1.0, 6.0, ((0, 4), (1, 8)), jnp.float32)
    onsite = jnp.clip(jax.random.uniform(key_of[1], (NORB,), jnp.float32, -1.0, 1.0) * levels(key_of[1], (NORB,), ((0, 8),), -0.4, 0.0), -1.0, 1.0)
    node_features = bell_draw(key_of[2], (ATOMS, FEAT), 1.0, 6.0, ((0, 8), (1, 4)))
    atom_orbitals = touch_ends(jax.random.randint(key_of[3], (ATOMS,), 4, 14), jax.random.fold_in(key_of[3], 1), 4, 13).astype(jnp.int32)
    pair_blocks = draw_pair_blocks(jax.random.fold_in(key_of[9], 71), 0)
    pair_live = draw_pair_live(jax.random.fold_in(key_of[9], 71), 0)
    weight_in = bell_draw(key_of[6], (FEAT, HID), FEAT ** -0.5, 0.25)
    bias_in = bell_draw(key_of[7], (HID,), 0.5, 3.0, (), jnp.float32)
    weight_out = bell_draw(key_of[8], (HID, OUTW), (HID * BO) ** -0.5, 0.009765625)
    return {"states_in": states_in, "onsite": onsite, "node_features": node_features, "atom_orbitals": atom_orbitals, "pair_blocks": pair_blocks, "pair_live": pair_live, "weight_in": weight_in, "bias_in": bias_in, "weight_out": weight_out}


def reference(states_in, onsite, node_features, atom_orbitals, pair_blocks, pair_live, weight_in, bias_in, weight_out):
    proj_blocks = jnp.dot(node_features, weight_in, preferred_element_type=jnp.float32).reshape(NB, ATOM_BLK, HID)
    orbital_valid = (jnp.arange(ORB)[None, :] < atom_orbitals[:, None]).astype(jnp.float32).reshape(NB, BO)

    def build_tile(pair_item):
        blocks_pair, live_flag = pair_item
        first_block = blocks_pair[0].astype(jnp.int32)
        second_block = blocks_pair[1].astype(jnp.int32)

        def compute(unused):
            first_proj = lax.dynamic_index_in_dim(proj_blocks, first_block, 0, keepdims=False)
            second_proj = lax.dynamic_index_in_dim(proj_blocks, second_block, 0, keepdims=False)
            hidden = jax.nn.silu(first_proj[:, None, :] + second_proj[None, :, :] + bias_in).astype(jnp.bfloat16)
            raw_tile = jnp.dot(hidden.reshape(ATOM_BLK * ATOM_BLK, HID), weight_out, preferred_element_type=jnp.float32)
            raw_tile = raw_tile.reshape(ATOM_BLK, ATOM_BLK, ORB, ORB).transpose(0, 2, 1, 3).reshape(BO, BO)
            first_valid = lax.dynamic_index_in_dim(orbital_valid, first_block, 0, keepdims=False)
            second_valid = lax.dynamic_index_in_dim(orbital_valid, second_block, 0, keepdims=False)
            return (raw_tile * (first_valid[:, None] * second_valid[None, :])).astype(jnp.bfloat16)

        def skipped(unused):
            return jnp.zeros((BO, BO), jnp.bfloat16)

        return lax.cond(live_flag > 0, compute, skipped, 0)

    tile_set = lax.map(build_tile, (pair_blocks, pair_live))

    def operate(vector):
        def add_pair(pair_number, running):
            first_start = (pair_blocks[pair_number, 0] * BO).astype(jnp.int32)
            second_start = (pair_blocks[pair_number, 1] * BO).astype(jnp.int32)

            def touch(current):
                tile_wide = tile_set[pair_number].astype(jnp.float32)
                first_field = lax.dynamic_slice_in_dim(vector, first_start, BO, 1)
                second_field = lax.dynamic_slice_in_dim(vector, second_start, BO, 1)
                first_sum = lax.dynamic_slice_in_dim(current, first_start, BO, 1) + lax.dot_general(
                    second_field, tile_wide, (((1,), (1,)), ((), ())), precision=lax.Precision.HIGHEST)
                current = lax.dynamic_update_slice_in_dim(current, first_sum, first_start, 1)
                second_sum = lax.dynamic_slice_in_dim(current, second_start, BO, 1) + jnp.dot(
                    first_field, tile_wide, precision=lax.Precision.HIGHEST)
                return lax.dynamic_update_slice_in_dim(current, second_sum, second_start, 1)

            return lax.cond(pair_live[pair_number] > 0, touch, lambda current: current, running)

        return lax.fori_loop(0, PAIRS, add_pair, vector * onsite[None, :])

    first_step = operate(states_in)
    second_step = 2.0 * operate(first_step) - states_in
    return first_step, second_step
```

```python
import functools

import jax
import jax.numpy as jnp
from jax import lax
from jax.experimental import pallas as pl
from jax.experimental.pallas import tpu as pltpu
from jax.sharding import PartitionSpec as P

ORB = 13
ATOM_BLK = 64
BO = ORB * ATOM_BLK
LANES = 128
PAD_ORB = 16
HALF = ATOM_BLK // 2
ROWS = HALF * PAD_ORB
COLS = ORB * LANES
WIDE = (ORB + 1) // 2 * LANES
STEP_ATOMS = 8
TILE_BYTES = ROWS * COLS * 2
VMEM_LIMIT = 60 * 1024 * 1024
CACHE_BUDGET = 38 * 1024 * 1024


def dot(left, right):
    return jnp.dot(left, right, preferred_element_type=jnp.float32)


def dot_t(left, right):
    return lax.dot_general(left, right, (((1,), (1,)), ((), ())), preferred_element_type=jnp.float32)


def onehot_matrix(rows, cols, match):
    row = lax.broadcasted_iota(jnp.int32, (rows, cols), 0)
    col = lax.broadcasted_iota(jnp.int32, (rows, cols), 1)
    return jnp.where(match(row, col), 1.0, 0.0).astype(jnp.bfloat16)


def natural_to_wide():
    return onehot_matrix(
        BO, WIDE, lambda n, l: (n == (l % ATOM_BLK) * ORB + l // ATOM_BLK) & (l < BO)
    )


def natural_to_split(parity):
    return onehot_matrix(
        BO,
        ROWS,
        lambda n, l: (n == (l // PAD_ORB * 2 + parity) * ORB + l % PAD_ORB) & (l % PAD_ORB < ORB),
    )


def split_to_natural(parity):
    return onehot_matrix(
        ROWS,
        BO,
        lambda l, n: (n == (l // PAD_ORB * 2 + parity) * ORB + l % PAD_ORB) & (l % PAD_ORB < ORB),
    )


def split_to_wide(parity):
    return onehot_matrix(
        ROWS,
        WIDE,
        lambda l, w: (w == (l % PAD_ORB) * ATOM_BLK + l // PAD_ORB * 2 + parity)
        & (l % PAD_ORB < ORB),
    )


def prepare_kernel(
    pair_count, block_count, place_ref, blocks_ref, live_ref, states_ref, onsite_ref, valid_ref,
    payload_ref, own_split_ref, tables_ref, counts_ref, slot_of, natural,
):
    me = place_ref[0]
    pairs = live_ref.shape[0]
    blocks = pair_count * block_count

    def clear(block, carry):
        slot_of[block] = -1
        return carry

    lax.fori_loop(0, blocks, clear, 0)

    def own_scan(end, carry):
        count, slots = carry
        pair, side = end // 2, end % 2
        target = blocks_ref[pair, side]
        source = blocks_ref[pair, 1 - side]
        wanted = (live_ref[pair] > 0) & (target // block_count == me)
        source_own = source // block_count == me
        fresh = wanted & jnp.logical_not(source_own) & (slot_of[source] < 0)

        @pl.when(fresh)
        def _():
            slot_of[source] = slots
            tables_ref[5, slots] = source

        @pl.when(wanted)
        def _():
            tables_ref[0, count] = target
            tables_ref[1, count] = source
            tables_ref[2, count] = side
            tables_ref[3, count] = target % block_count
            tables_ref[4, count] = jnp.where(
                source_own, 2 * pairs + source % block_count, slot_of[source]
            )

        return (count + wanted.astype(jnp.int32), slots + fresh.astype(jnp.int32))

    own_total, slot_total = lax.fori_loop(0, 2 * pairs, own_scan, (0, 0))

    def next_scan(end, count):
        pair, side = end // 2, end % 2
        target = blocks_ref[pair, side]
        source = blocks_ref[pair, 1 - side]
        wanted = (live_ref[pair] > 0) & (slot_of[target] >= 0) & (source // block_count != me)

        @pl.when(wanted)
        def _():
            tables_ref[0, count] = target
            tables_ref[1, count] = source
            tables_ref[2, count] = side
            tables_ref[3, count] = slot_of[target]
            tables_ref[4, count] = 0

        return count + wanted.astype(jnp.int32)

    total = lax.fori_loop(0, 2 * pairs, next_scan, own_total)
    counts_ref[0] = own_total
    counts_ref[1] = total
    counts_ref[2] = slot_total

    state_rows = states_ref.shape[0]
    extra = block_count * state_rows
    onsite_rows = []
    valid_rows = []
    for block in range(block_count):
        cut = slice(block * BO, (block + 1) * BO)
        valid = valid_ref[:, cut]
        natural[block * state_rows : (block + 1) * state_rows, :] = (
            states_ref[:, cut] * valid
        ).astype(jnp.bfloat16)
        onsite_rows.append(onsite_ref[:, cut] * valid)
        valid_rows.append(valid)
    natural[extra:, :] = jnp.concatenate(onsite_rows + valid_rows, axis=0).astype(jnp.bfloat16)
    payload_ref[...] = dot(natural[...], natural_to_wide()).astype(jnp.bfloat16)
    for parity in range(2):
        split = dot(natural[:extra, :], natural_to_split(parity)).astype(jnp.bfloat16)
        for block in range(block_count):
            own_split_ref[block, parity * state_rows : (parity + 1) * state_rows, :] = split[
                block * state_rows : (block + 1) * state_rows, :
            ]


def spread_states(fields):
    wide = fields.astype(jnp.float32)
    low = lax.broadcasted_iota(jnp.int32, (wide.shape[0], LANES), 1) < ATOM_BLK
    even, odd = [], []
    for column in range(WIDE // LANES):
        part = wide[:, column * LANES : (column + 1) * LANES]
        swapped = pltpu.roll(part, ATOM_BLK, 1)
        even += [jnp.where(low, part, 0.0), jnp.where(low, swapped, 0.0)]
        odd += [jnp.where(low, 0.0, swapped), jnp.where(low, 0.0, part)]
    return jnp.concatenate(
        [jnp.concatenate(even[:ORB], axis=1), jnp.concatenate(odd[:ORB], axis=1)], axis=0
    ).astype(jnp.bfloat16)


def fold_products(products):
    low = lax.broadcasted_iota(jnp.int32, (products.shape[0], LANES), 1) < ATOM_BLK
    sums = []
    for orbital in range(ORB):
        part = products[:, orbital * LANES : (orbital + 1) * LANES]
        sums.append(part + pltpu.roll(part, ATOM_BLK, 1))
    sums.append(jnp.zeros_like(sums[0]))
    return jnp.concatenate(
        [jnp.where(low, sums[2 * c], sums[2 * c + 1]) for c in range(WIDE // LANES)], axis=1
    )


def filter_kernel(
    cache, block_count, place_ref, tables_ref, counts_ref, features_ref, fields_ref, own_split_ref,
    states_ref, onsite_ref, valid_ref, weight_in_ref, bias_ref, weight_out_ref,
    first_ref, second_ref,
    tiles, proj_target, proj_source, hidden, own_sums, again_sums, back_sums, next_sums, moved,
):
    own_total = counts_ref[0]
    total = counts_ref[1]
    state_rows = states_ref.shape[0]
    pairs2 = tables_ref.shape[1]
    slots = back_sums.shape[0]
    own_sums[...] = jnp.zeros_like(own_sums)
    again_sums[...] = jnp.zeros_like(again_sums)
    back_sums[...] = jnp.zeros_like(back_sums)
    next_sums[...] = jnp.zeros_like(next_sums)

    def build_tile(task, keep):
        target = tables_ref[0, task]
        source = tables_ref[1, task]
        side = tables_ref[2, task]
        target_proj = dot(features_ref[target], weight_in_ref[...])
        proj_target[...] = (0.5 * (target_proj + bias_ref[...])).reshape(proj_target.shape)
        proj_source[...] = 0.5 * dot(features_ref[source], weight_in_ref[...])
        weight = weight_out_ref[side]

        def chunk(index, carry):
            targets = proj_target[index]
            for atom in range(STEP_ATOMS):
                half = targets[atom : atom + 1, :] + proj_source[...]
                hidden[atom * ATOM_BLK : (atom + 1) * ATOM_BLK, :] = (
                    half + half * jnp.tanh(half)
                ).astype(jnp.bfloat16)
            raw = dot_t(weight, hidden[...]).astype(jnp.bfloat16)
            for couple in range(STEP_ATOMS // 2):
                row = (index * (STEP_ATOMS // 2) + couple) * PAD_ORB
                for orbital in range(ORB):
                    tiles[
                        keep,
                        pl.ds(pl.multiple_of(row, PAD_ORB), PAD_ORB),
                        orbital * LANES : (orbital + 1) * LANES,
                    ] = raw[
                        orbital * PAD_ORB : (orbital + 1) * PAD_ORB,
                        couple * LANES : (couple + 1) * LANES,
                    ]
            return carry

        lax.fori_loop(0, ATOM_BLK // STEP_ATOMS, chunk, 0)

    def fields_of(block):
        return fields_ref[block // block_count, block % block_count]

    def first_pass(task, carry):
        keep = jnp.minimum(task, cache)
        build_tile(task, keep)
        where = tables_ref[3, task]
        spread = spread_states(fields_of(tables_ref[1, task]))
        arrived = dot_t(spread, tiles[keep])

        @pl.when(task < own_total)
        def _():
            own_sums[where] += arrived
            slot = tables_ref[4, task]

            @pl.when(slot < pairs2)
            def _():
                back = dot(own_split_ref[where], tiles[keep])
                low = lax.broadcasted_iota(jnp.int32, (state_rows, COLS), 1) % LANES < ATOM_BLK
                back_sums[slot] += jnp.where(low, back[:state_rows], back[state_rows:])

        @pl.when(task >= own_total)
        def _():
            next_sums[where] += arrived

        return carry

    lax.fori_loop(0, total, first_pass, 0)

    def to_layout(sums, matrix):
        groups = sums.shape[0]
        result = 0.0
        for parity in range(2):
            rows = sums[:, parity * state_rows : (parity + 1) * state_rows, :]
            rows = rows.reshape(groups * state_rows, ROWS).astype(jnp.bfloat16)
            result = result + dot(rows, matrix(parity))
        return result

    moved_own = to_layout(own_sums[...], split_to_natural)
    own_rows = []
    for block in range(block_count):
        cut = slice(block * BO, (block + 1) * BO)
        valid = valid_ref[:, cut]
        new = (
            states_ref[:, cut] * onsite_ref[:, cut]
            + moved_own[block * state_rows : (block + 1) * state_rows] * valid
        )
        first_ref[:, cut] = new
        own_rows.append((new * valid).astype(jnp.bfloat16))
    own_wide = dot(jnp.concatenate(own_rows, axis=0), natural_to_wide()).astype(jnp.bfloat16)
    for block in range(block_count):
        moved[slots + block] = own_wide[block * state_rows : (block + 1) * state_rows]
    moved_next = to_layout(next_sums[...], split_to_wide)
    for slot in range(slots):

        @pl.when(slot < counts_ref[2])
        def _():
            block = tables_ref[5, slot]
            owner = block // block_count
            local = block % block_count
            extras = fields_ref[owner, block_count].astype(jnp.float32)
            row = lax.broadcasted_iota(jnp.int32, extras.shape, 0)
            onsite = jnp.sum(jnp.where(row == local, extras, 0.0), axis=0, keepdims=True)
            valid = jnp.sum(
                jnp.where(row == local + block_count, extras, 0.0), axis=0, keepdims=True
            )
            products = moved_next[slot * state_rows : (slot + 1) * state_rows] + fold_products(
                back_sums[slot]
            )
            moved[slot] = (
                fields_ref[owner, local].astype(jnp.float32) * onsite + products * valid
            ).astype(jnp.bfloat16)

    def second_pass(task, carry):
        keep = jnp.minimum(task, cache)

        @pl.when(task >= cache)
        def _():
            build_tile(task, keep)

        slot = tables_ref[4, task]
        slot = jnp.where(slot >= pairs2, slot - pairs2 + slots, slot)
        again_sums[tables_ref[3, task]] += dot_t(spread_states(moved[slot]), tiles[keep])
        return carry

    lax.fori_loop(0, own_total, second_pass, 0)
    moved_again = to_layout(again_sums[...], split_to_natural)
    for block in range(block_count):
        cut = slice(block * BO, (block + 1) * BO)
        second_ref[:, cut] = (
            2.0
            * (
                first_ref[:, cut] * onsite_ref[:, cut]
                + moved_again[block * state_rows : (block + 1) * state_rows] * valid_ref[:, cut]
            )
            - states_ref[:, cut]
        )


def per_device(
    states_in, onsite, node_features, atom_orbitals, pair_blocks, pair_live, weight_in, bias_in,
    weight_out,
):
    pair_count = lax.axis_size("pair")
    state_rows = states_in.shape[0]
    block_count = onsite.shape[0] // BO
    blocks = pair_count * block_count
    pairs = pair_live.shape[0]
    pairs_here = pairs // pair_count
    end_count = 2 * pairs_here
    slots = pair_count * ((end_count + pair_count - 1) // pair_count)
    hid = weight_in.shape[1]
    feat = weight_in.shape[0]
    place = lax.axis_index("pair").astype(jnp.int32).reshape(1)
    atoms_here = node_features.shape[0]
    own_orbitals = lax.dynamic_slice_in_dim(atom_orbitals, place[0] * atoms_here, atoms_here)
    valid = (jnp.arange(ORB)[None, :] < own_orbitals[:, None]).astype(jnp.float32)
    valid = valid.reshape(1, atoms_here * ORB)
    onsite_row = onsite.reshape(1, -1)
    cube = weight_out.reshape(hid, ORB, ORB).astype(jnp.float32)
    pad = ((0, 0), (0, PAD_ORB - ORB), (0, 0))
    weights = jnp.stack(
        [
            jnp.pad(cube.transpose(2, 1, 0), pad).reshape(ORB * PAD_ORB, hid),
            jnp.pad(cube.transpose(1, 2, 0), pad).reshape(ORB * PAD_ORB, hid),
        ]
    ).astype(jnp.bfloat16)

    smem = pl.BlockSpec(memory_space=pltpu.SMEM)
    vmem = pl.BlockSpec(memory_space=pltpu.VMEM)
    groups = block_count + (2 * block_count + state_rows - 1) // state_rows
    payload, own_split, tables, counts = pl.pallas_call(
        functools.partial(prepare_kernel, pair_count, block_count),
        out_shape=[
            jax.ShapeDtypeStruct((groups * state_rows, WIDE), jnp.bfloat16),
            jax.ShapeDtypeStruct((block_count, 2 * state_rows, ROWS), jnp.bfloat16),
            jax.ShapeDtypeStruct((6, 2 * pairs), jnp.int32),
            jax.ShapeDtypeStruct((3,), jnp.int32),
        ],
        in_specs=[smem, smem, smem, vmem, vmem, vmem],
        out_specs=[vmem, vmem, smem, smem],
        scratch_shapes=[
            pltpu.SMEM((blocks,), jnp.int32),
            pltpu.VMEM((groups * state_rows, BO), jnp.bfloat16),
        ],
        compiler_params=pltpu.CompilerParams(vmem_limit_bytes=VMEM_LIMIT),
        name="prepare",
    )(place, pair_blocks, pair_live, states_in, onsite_row, valid)

    features = lax.all_gather(node_features, "pair", axis=0, tiled=True)
    features = lax.all_gather(features, "state", axis=1, tiled=True)
    features = features.reshape(blocks, ATOM_BLK, feat)
    fields = lax.all_gather(payload, "pair", axis=0, tiled=True)
    fields = fields.reshape(pair_count, groups, state_rows, WIDE)
    held = features.size * 2 + fields.size * 2
    cache = max(1, min(slots, (CACHE_BUDGET - held) // TILE_BYTES))
    return pl.pallas_call(
        functools.partial(filter_kernel, cache, block_count),
        out_shape=[jax.ShapeDtypeStruct(states_in.shape, jnp.float32)] * 2,
        in_specs=[smem] * 3 + [vmem] * 9,
        out_specs=[vmem, vmem],
        scratch_shapes=[
            pltpu.VMEM((cache + 1, ROWS, COLS), jnp.bfloat16),
            pltpu.VMEM((ATOM_BLK // STEP_ATOMS, STEP_ATOMS, hid), jnp.float32),
            pltpu.VMEM((ATOM_BLK, hid), jnp.float32),
            pltpu.VMEM((STEP_ATOMS * ATOM_BLK, hid), jnp.bfloat16),
            pltpu.VMEM((block_count, 2 * state_rows, ROWS), jnp.float32),
            pltpu.VMEM((block_count, 2 * state_rows, ROWS), jnp.float32),
            pltpu.VMEM((slots, state_rows, COLS), jnp.float32),
            pltpu.VMEM((slots, 2 * state_rows, ROWS), jnp.float32),
            pltpu.VMEM((slots + block_count, state_rows, WIDE), jnp.bfloat16),
        ],
        compiler_params=pltpu.CompilerParams(vmem_limit_bytes=VMEM_LIMIT),
        name="filter",
    )(
        place, tables, counts, features, fields, own_split, states_in, onsite_row, valid,
        weight_in, bias_in.reshape(1, hid), weights,
    )


def solution(mesh):
    return jax.shard_map(
        per_device,
        mesh=mesh,
        in_specs=(P("state", "pair"), P("pair"), P("pair", "state"), P(), P(), P(), P(), P(), P()),
        out_specs=(P("state", "pair"), P("state", "pair")),
        check_vma=False,
    )
```

```python
import functools

import jax
import jax.numpy as jnp
from jax import lax
from jax.experimental import pallas as pl
from jax.experimental.pallas import tpu as pltpu
from jax.sharding import PartitionSpec as P

ORB = 13
ATOM_BLK = 64
BO = ORB * ATOM_BLK
LANES = 128
PAD_ORB = 16
HALF = ATOM_BLK // 2
ROWS = HALF * PAD_ORB
COLS = ORB * LANES
WIDE = (ORB + 1) // 2 * LANES
STEP_ATOMS = 8
SLOT_GROUP = 8
TILE_BYTES = ROWS * COLS * 2
VMEM_LIMIT = 60 * 1024 * 1024
CACHE_BUDGET = 44 * 1024 * 1024


def dot(left, right):
    return jnp.dot(left, right, preferred_element_type=jnp.float32)


def dot_t(left, right):
    return lax.dot_general(left, right, (((1,), (1,)), ((), ())), preferred_element_type=jnp.float32)


def onehot_columns(rows, cols, row_of_col):
    col = lax.broadcasted_iota(jnp.int32, (1, cols), 1)
    row = lax.broadcasted_iota(jnp.int32, (rows, cols), 0)
    return jnp.where(row == row_of_col(col), 1.0, 0.0).astype(jnp.bfloat16)


def onehot_rows(rows, cols, col_of_row):
    row = lax.broadcasted_iota(jnp.int32, (rows, 1), 0)
    col = lax.broadcasted_iota(jnp.int32, (rows, cols), 1)
    return jnp.where(col == col_of_row(row), 1.0, 0.0).astype(jnp.bfloat16)


def natural_of_wide(lane):
    return jnp.where(lane < BO, lane % ATOM_BLK * ORB + lane // ATOM_BLK, -1)


def natural_of_split(parity, lane):
    orbital = lane % PAD_ORB
    return jnp.where(orbital < ORB, (lane // PAD_ORB * 2 + parity) * ORB + orbital, -1)


def wide_of_split(parity, lane):
    orbital = lane % PAD_ORB
    return jnp.where(orbital < ORB, orbital * ATOM_BLK + lane // PAD_ORB * 2 + parity, -1)


def natural_to_wide():
    return onehot_columns(BO, WIDE, natural_of_wide)


def natural_to_split(parity):
    return onehot_columns(BO, ROWS, functools.partial(natural_of_split, parity))


def split_to_natural(parity):
    return onehot_rows(ROWS, BO, functools.partial(natural_of_split, parity))


def split_to_wide(parity):
    return onehot_rows(ROWS, WIDE, functools.partial(wide_of_split, parity))


def as_row(column, eye):
    return jnp.sum(jnp.where(eye, column, 0), axis=0, keepdims=True)


def tables_kernel(pair_count, block_count, place_ref, blocks_ref, live_ref, tables_ref):
    me = place_ref[0]
    core = place_ref[1].astype(jnp.float32)
    pairs = blocks_ref.shape[0]
    ends = 2 * pairs
    blocks = pair_count * block_count
    eye = lax.broadcasted_iota(jnp.int32, (pairs, pairs), 0) == lax.broadcasted_iota(
        jnp.int32, (pairs, pairs), 1
    )
    firsts = as_row(blocks_ref[:, 0:1], eye)
    seconds = as_row(blocks_ref[:, 1:2], eye)
    target = jnp.concatenate([firsts, seconds], axis=1)
    source = jnp.concatenate([seconds, firsts], axis=1)
    live = jnp.concatenate([live_ref[...], live_ref[...]], axis=1) > 0
    lane = lax.broadcasted_iota(jnp.int32, (1, ends), 1)
    source_own = source // block_count == me
    own = live & (target // block_count == me)

    def number(flag):
        return jnp.where(flag, 1.0, 0.0)

    def whole(value):
        return value.astype(jnp.bfloat16)

    row = lax.broadcasted_iota(jnp.int32, (blocks, ends), 0)
    below = whole(
        number(
            lax.broadcasted_iota(jnp.int32, (blocks, blocks), 1)
            < lax.broadcasted_iota(jnp.int32, (blocks, blocks), 0)
        )
    )

    def before(column):
        return dot(below, whole(jnp.broadcast_to(column, (blocks, LANES))))[:, 0:1]

    def at(flag, column):
        return jnp.sum(jnp.where(flag, column, 0.0), axis=0, keepdims=True)

    is_source = row == source
    is_target = row == target
    own_ends = jnp.sum(number(is_source & own), axis=1, keepdims=True)
    has = number(own_ends > 0)
    following = live & (at(is_target, has) > 0) & jnp.logical_not(source_own)
    work = jnp.where(
        has > 0,
        3.0 * own_ends + 2.0 * jnp.sum(number(is_target & following), axis=1, keepdims=True),
        0.0,
    )
    work_total = jnp.sum(jnp.broadcast_to(work, (blocks, LANES)), axis=0, keepdims=True)[:, 0:1]
    half = number(2.0 * before(work) + work > work_total)
    mine = has * number(half == core)
    slot = before(mine)
    slot_total = jnp.sum(jnp.broadcast_to(mine, (blocks, LANES)), axis=0, keepdims=True)[:, 0:1]
    source_slot = at(is_source, slot)
    target_slot = at(is_target, slot)
    own = own & (at(is_source, mine) > 0)
    following = following & (at(is_target, mine) > 0)
    earlier = whole(
        number(
            lax.broadcasted_iota(jnp.int32, (ends, ends), 0)
            < lax.broadcasted_iota(jnp.int32, (ends, ends), 1)
        )
    )
    flags = jnp.concatenate(
        [number(own), number(following), jnp.zeros((6, ends), jnp.float32)], axis=0
    )
    ranks = dot(whole(flags), earlier)
    own_total = jnp.sum(number(own), axis=1, keepdims=True)
    total = own_total + jnp.sum(number(following), axis=1, keepdims=True)
    own_rank = jnp.where(own, ranks[0:1], -1.0)
    next_rank = jnp.where(following, own_total + ranks[1:2], -1.0)

    def position(block):
        return ((block // block_count) ^ me) * block_count + block % block_count

    def fields(where, slots):
        rows = [
            position(target).astype(jnp.float32),
            position(source).astype(jnp.float32),
            number(lane >= pairs),
            where,
            slots,
        ]
        return whole(jnp.concatenate(rows + [jnp.zeros((3, ends), jnp.float32)], axis=0))

    spot = lax.broadcasted_iota(jnp.int32, (ends, ends), 0).astype(jnp.float32)
    placed = dot_t(
        fields((target % block_count).astype(jnp.float32), source_slot),
        whole(number(spot == own_rank)),
    ) + dot_t(fields(target_slot, target_slot), whole(number(spot == next_rank)))
    block_row = lax.broadcasted_iota(jnp.int32, (8, blocks), 1)
    slot_place = number(
        (lax.broadcasted_iota(jnp.int32, (blocks, ends), 1).astype(jnp.float32) == slot) & (mine > 0)
    )
    slot_block = dot(whole(position(block_row).astype(jnp.float32)), whole(slot_place))
    totals = jnp.where(
        lane == 0, own_total, jnp.where(lane == 1, total, jnp.where(lane == 2, slot_total, 0.0))
    )
    tables_ref[...] = jnp.concatenate(
        [placed[0:5], slot_block[0:1], totals, jnp.zeros((1, ends), jnp.float32)], axis=0
    ).astype(jnp.int32)


def prepare_kernel(
    block_count, states_ref, onsite_ref, valid_ref, payload_ref, own_split_ref, natural
):
    state_rows = states_ref.shape[0]
    extra = block_count * state_rows
    onsite_rows = []
    valid_rows = []
    for block in range(block_count):
        cut = slice(block * BO, (block + 1) * BO)
        valid = valid_ref[:, cut]
        natural[block * state_rows : (block + 1) * state_rows, :] = (
            states_ref[:, cut] * valid
        ).astype(jnp.bfloat16)
        onsite_rows.append(onsite_ref[:, cut] * valid)
        valid_rows.append(valid)
    natural[extra:, :] = jnp.concatenate(onsite_rows + valid_rows, axis=0).astype(jnp.bfloat16)
    payload_ref[...] = dot(natural[...], natural_to_wide()).astype(jnp.bfloat16)
    for parity in range(2):
        split = dot(natural[:extra, :], natural_to_split(parity)).astype(jnp.bfloat16)
        for block in range(block_count):
            own_split_ref[block, parity * state_rows : (parity + 1) * state_rows, :] = split[
                block * state_rows : (block + 1) * state_rows, :
            ]


def spread_states(fields):
    wide = fields.astype(jnp.float32)
    low = lax.broadcasted_iota(jnp.int32, (wide.shape[0], LANES), 1) < ATOM_BLK
    even, odd = [], []
    for column in range(WIDE // LANES):
        part = wide[:, column * LANES : (column + 1) * LANES]
        swapped = pltpu.roll(part, ATOM_BLK, 1)
        even += [jnp.where(low, part, 0.0), jnp.where(low, swapped, 0.0)]
        odd += [jnp.where(low, 0.0, swapped), jnp.where(low, 0.0, part)]
    return jnp.concatenate(
        [jnp.concatenate(even[:ORB], axis=1), jnp.concatenate(odd[:ORB], axis=1)], axis=0
    ).astype(jnp.bfloat16)


def fold_products(products):
    low = lax.broadcasted_iota(jnp.int32, (products.shape[0], LANES), 1) < ATOM_BLK
    sums = []
    for orbital in range(ORB):
        part = products[:, orbital * LANES : (orbital + 1) * LANES]
        sums.append(part + pltpu.roll(part, ATOM_BLK, 1))
    sums.append(jnp.zeros_like(sums[0]))
    return jnp.concatenate(
        [jnp.where(low, sums[2 * c], sums[2 * c + 1]) for c in range(WIDE // LANES)], axis=1
    )


def filter_kernel(
    cache, block_count, places, tables_ref, own_split_ref, other_split_ref, weight_in_ref, bias_ref,
    weight_out_ref, *refs
):
    count = len(places)
    pieces = refs[:count]
    arrivals = refs[count:-15]
    (
        kept_ref, sent_ref, features_ref, fields_ref, feature_sems, field_sems,
        tiles, proj_target, proj_source, hidden, own_sums, again_sums, back_sums, next_sums, moved,
    ) = refs[-15:]
    state_rows = kept_ref.shape[1]
    copies = []
    for index, (piece, (start, rows, first, column)) in enumerate(zip(pieces, places)):
        copies.append(
            pltpu.make_async_copy(
                piece.at[start : start + rows],
                features_ref.at[first : first + rows, :, column : column + piece.shape[2]],
                feature_sems.at[index],
            )
        )
    for index, arrival in enumerate(arrivals):
        first = index // 2 * 2
        rows = slice(index % 2 * state_rows, (index % 2 + 1) * state_rows)
        copies.append(
            pltpu.make_async_copy(
                arrival, fields_ref.at[first : first + 2, :, rows], field_sems.at[index]
            )
        )
    for copy in copies:
        copy.start()
    own_total = tables_ref[6, 0]
    total = tables_ref[6, 1]
    both = 2 * state_rows
    slots = back_sums.shape[0]
    own_sums[...] = jnp.zeros_like(own_sums)
    again_sums[...] = jnp.zeros_like(again_sums)
    back_sums[...] = jnp.zeros_like(back_sums)
    next_sums[...] = jnp.zeros_like(next_sums)
    for copy in copies:
        copy.wait()

    def build_tile(task, keep):
        target = tables_ref[0, task]
        source = tables_ref[1, task]
        side = tables_ref[2, task]
        target_proj = dot(features_ref[target], weight_in_ref[...])
        proj_target[...] = (0.5 * (target_proj + bias_ref[...])).reshape(proj_target.shape)
        proj_source[...] = 0.5 * dot(features_ref[source], weight_in_ref[...])
        weight = weight_out_ref[side]

        def chunk(index, carry):
            targets = proj_target[index]
            for atom in range(STEP_ATOMS):
                half = targets[atom : atom + 1, :] + proj_source[...]
                hidden[atom * ATOM_BLK : (atom + 1) * ATOM_BLK, :] = (
                    half + half * jnp.tanh(half)
                ).astype(jnp.bfloat16)
            raw = dot_t(hidden[...], weight).astype(jnp.bfloat16).T
            for couple in range(STEP_ATOMS // 2):
                row = (index * (STEP_ATOMS // 2) + couple) * PAD_ORB
                for orbital in range(ORB):
                    tiles[
                        keep,
                        pl.ds(pl.multiple_of(row, PAD_ORB), PAD_ORB),
                        orbital * LANES : (orbital + 1) * LANES,
                    ] = raw[
                        orbital * PAD_ORB : (orbital + 1) * PAD_ORB,
                        couple * LANES : (couple + 1) * LANES,
                    ]
            return carry

        lax.fori_loop(0, ATOM_BLK // STEP_ATOMS, chunk, 0, unroll=True)

    def fields_of(block):
        return fields_ref[block // block_count, block % block_count]

    def first_pass(task, carry):
        keep = jnp.minimum(task, cache)
        build_tile(task, keep)
        where = tables_ref[3, task]
        spread = spread_states(fields_of(tables_ref[1, task]))
        arrived = dot_t(spread, tiles[keep])

        @pl.when(task < own_total)
        def _():
            own_sums[where] += arrived
            fields = jnp.concatenate(
                [
                    split[where, parity * state_rows : (parity + 1) * state_rows]
                    for parity in range(2)
                    for split in (own_split_ref, other_split_ref)
                ],
                axis=0,
            )
            back = dot(fields, tiles[keep])
            low = lax.broadcasted_iota(jnp.int32, (both, COLS), 1) % LANES < ATOM_BLK
            back_sums[tables_ref[4, task]] += jnp.where(low, back[:both], back[both:])

        @pl.when(task >= own_total)
        def _():
            next_sums[where] += arrived

        return carry

    lax.fori_loop(0, total, first_pass, 0)

    def to_layout(sums, matrix):
        groups = sums.shape[0]
        result = 0.0
        for parity in range(2):
            rows = sums[:, parity * both : (parity + 1) * both, :]
            rows = rows.reshape(groups * both, ROWS).astype(jnp.bfloat16)
            result = result + dot(rows, matrix(parity))
        return result

    def put(step, sums):
        natural = to_layout(sums, split_to_natural)
        for block in range(block_count):
            cut = slice(block * BO, (block + 1) * BO)
            middle = block * both + state_rows
            kept_ref[step, :, cut] = natural[block * both : middle]
            sent_ref[step, :, cut] = natural[middle : (block + 1) * both].astype(jnp.bfloat16)

    put(0, own_sums[...])
    for start in range(0, slots, SLOT_GROUP):

        @pl.when(start < tables_ref[6, 2])
        def _():
            moved_next = to_layout(next_sums[start : start + SLOT_GROUP], split_to_wide)
            for slot in range(start, min(start + SLOT_GROUP, slots)):
                block = tables_ref[5, slot]
                owner = block // block_count
                local = block % block_count
                extras = fields_ref[owner, block_count, :state_rows].astype(jnp.float32)
                row = lax.broadcasted_iota(jnp.int32, extras.shape, 0)
                onsite = jnp.sum(jnp.where(row == local, extras, 0.0), axis=0, keepdims=True)
                valid = jnp.sum(
                    jnp.where(row == local + block_count, extras, 0.0), axis=0, keepdims=True
                )
                part = (slot - start) * both
                products = moved_next[part : part + both] + fold_products(back_sums[slot])
                moved[slot] = (
                    fields_ref[owner, local].astype(jnp.float32) * onsite + products * valid
                ).astype(jnp.bfloat16)

    def second_pass(task, carry):
        keep = jnp.minimum(task, cache)

        @pl.when(task >= cache)
        def _():
            build_tile(task, keep)

        slot = tables_ref[4, task]
        again_sums[tables_ref[3, task]] += dot_t(spread_states(moved[slot]), tiles[keep])
        return carry

    lax.fori_loop(0, own_total, second_pass, 0)
    put(1, again_sums[...])


def finish_kernel(states_ref, onsite_ref, valid_ref, kept_ref, got_ref, first_ref, second_ref):
    states = states_ref[...]
    onsite = onsite_ref[...]
    valid = valid_ref[...]
    first = states * onsite + (kept_ref[0] + got_ref[0].astype(jnp.float32)) * valid
    first_ref[...] = first
    again = (kept_ref[1] + got_ref[1].astype(jnp.float32)) * valid
    second_ref[...] = 2.0 * (first * onsite + again) - states


def swap(value, axis, offset):
    size = lax.axis_size(axis)
    return lax.ppermute(value, axis, [(index, index ^ offset) for index in range(size)])


def after(value, *earlier):
    return lax.optimization_barrier((value, *earlier))[0]


def far_entries(value):
    entries = {0: value}
    bit = lax.axis_size("pair") // 2
    while bit > 1:
        entries.update({old ^ bit: swap(entry, "pair", bit) for old, entry in entries.items()})
        bit //= 2
    return entries


def gather_all(features, payload):
    atoms, quarter = features.shape
    far = far_entries(features)
    offsets = sorted(far)
    payload = after(payload, *[far[offset] for offset in offsets[1:]])
    pieces, places = [], []
    for offset in offsets:
        both = jnp.concatenate([far[offset], swap(far[offset], "pair", 1)], axis=0)
        bundle = [both]
        for part in range(2, lax.axis_size("state"), 2):
            bundle.append(swap(both, "state", part))
        rows = both.shape[0]
        bundle = jnp.concatenate(bundle, axis=0)
        other = swap(bundle, "state", 1)
        for part in range(bundle.shape[0] // rows):
            cut = slice(part * rows, (part + 1) * rows)
            couple = [(bundle, part * rows), (other, part * rows)]
            if quarter % LANES:
                couple = [(jnp.concatenate([bundle[cut], other[cut]], axis=1), 0)]
            for side, (piece, start) in enumerate(couple):
                pieces.append(piece)
                places.append((start, rows, offset * atoms, (2 * part + side) * quarter))
    far = far_entries(payload)
    fields = []
    for offset in offsets:
        both = jnp.stack([far[offset], swap(far[offset], "pair", 1)])
        fields += [both, swap(both, "state", 1)]
    return pieces, places, fields


def run_filter(
    places, blocks, slots, tables, own_split, other_split, weights_here, bias_row, weights, pieces,
    fields,
):
    feat, hid = weights_here.shape
    pair_count = len(fields)
    _, groups, state_rows, _ = fields[0].shape
    block_count = blocks // pair_count
    both = 2 * state_rows
    held = blocks * ATOM_BLK * feat * 2 + pair_count * fields[0].size * 2
    held += slots * both * (COLS + 2 * ROWS) * 4
    cache = max(1, min(slots, (CACHE_BUDGET - held) // TILE_BYTES))
    smem = pl.BlockSpec(memory_space=pltpu.SMEM)
    vmem = pl.BlockSpec(memory_space=pltpu.VMEM)
    hbm = pl.BlockSpec(memory_space=pl.ANY)
    partial = (2, state_rows, block_count * BO)
    return pl.pallas_call(
        functools.partial(filter_kernel, cache, block_count, places),
        out_shape=[
            jax.ShapeDtypeStruct(partial, jnp.float32),
            jax.ShapeDtypeStruct(partial, jnp.bfloat16),
        ],
        in_specs=[smem] + [vmem] * 5 + [hbm] * (len(pieces) + len(fields)),
        out_specs=[vmem, vmem],
        scratch_shapes=[
            pltpu.VMEM((blocks, ATOM_BLK, feat), jnp.bfloat16),
            pltpu.VMEM((pair_count, groups, both, WIDE), jnp.bfloat16),
            pltpu.SemaphoreType.DMA((len(pieces),)),
            pltpu.SemaphoreType.DMA((len(fields),)),
            pltpu.VMEM((cache + 1, ROWS, COLS), jnp.bfloat16),
            pltpu.VMEM((ATOM_BLK // STEP_ATOMS, STEP_ATOMS, hid), jnp.float32),
            pltpu.VMEM((ATOM_BLK, hid), jnp.float32),
            pltpu.VMEM((STEP_ATOMS * ATOM_BLK, hid), jnp.bfloat16),
            pltpu.VMEM((block_count, 2 * both, ROWS), jnp.float32),
            pltpu.VMEM((block_count, 2 * both, ROWS), jnp.float32),
            pltpu.VMEM((slots, both, COLS), jnp.float32),
            pltpu.VMEM((slots, 2 * both, ROWS), jnp.float32),
            pltpu.VMEM((slots, both, WIDE), jnp.bfloat16),
        ],
        compiler_params=pltpu.CompilerParams(vmem_limit_bytes=VMEM_LIMIT),
        name="filter",
    )(
        tables, own_split, other_split, weights_here, bias_row, weights, *pieces, *fields,
    )


def per_device(
    states_in, onsite, node_features, atom_orbitals, pair_blocks, pair_live, weight_in, bias_in,
    weight_out,
):
    pair_count = lax.axis_size("pair")
    state_rows = states_in.shape[0]
    block_count = onsite.shape[0] // BO
    blocks = pair_count * block_count
    pairs = pair_live.shape[0]
    pairs_here = pairs // pair_count
    end_count = 2 * pairs_here
    slots = pair_count * ((end_count + pair_count - 1) // pair_count)
    hid = weight_in.shape[1]
    feat = weight_in.shape[0]
    place = jnp.stack([lax.axis_index("pair"), lax.axis_index("state") % 2]).astype(jnp.int32)
    atoms_here = node_features.shape[0]
    own_orbitals = lax.dynamic_slice_in_dim(atom_orbitals, place[0] * atoms_here, atoms_here)
    valid = (jnp.arange(ORB)[None, :] < own_orbitals[:, None]).astype(jnp.float32)
    valid = valid.reshape(1, atoms_here * ORB)
    onsite_row = onsite.reshape(1, -1)
    cube = weight_out.reshape(hid, ORB, ORB).astype(jnp.float32)
    pad = ((0, 0), (0, PAD_ORB - ORB), (0, 0))
    weights = jnp.stack(
        [
            jnp.pad(cube.transpose(2, 1, 0), pad).reshape(ORB * PAD_ORB, hid),
            jnp.pad(cube.transpose(1, 2, 0), pad).reshape(ORB * PAD_ORB, hid),
        ]
    ).astype(jnp.bfloat16)

    smem = pl.BlockSpec(memory_space=pltpu.SMEM)
    vmem = pl.BlockSpec(memory_space=pltpu.VMEM)
    hbm = pl.BlockSpec(memory_space=pl.ANY)
    groups = block_count + (2 * block_count + state_rows - 1) // state_rows
    limit = pltpu.CompilerParams(vmem_limit_bytes=VMEM_LIMIT)
    payload, own_split = pl.pallas_call(
        functools.partial(prepare_kernel, block_count),
        out_shape=[
            jax.ShapeDtypeStruct((groups * state_rows, WIDE), jnp.bfloat16),
            jax.ShapeDtypeStruct((block_count, 2 * state_rows, ROWS), jnp.bfloat16),
        ],
        in_specs=[vmem, vmem, vmem],
        out_specs=[vmem, vmem],
        scratch_shapes=[pltpu.VMEM((groups * state_rows, BO), jnp.bfloat16)],
        compiler_params=limit,
        name="prepare",
    )(states_in, onsite_row, valid)
    pieces, places, fields = gather_all(
        node_features, payload.reshape(groups, state_rows, WIDE)
    )
    pieces = [piece.reshape(-1, ATOM_BLK, piece.shape[1]) for piece in pieces]
    places = [
        (start // ATOM_BLK, rows // ATOM_BLK, first // ATOM_BLK, column)
        for start, rows, first, column in places
    ]
    tables = pl.pallas_call(
        functools.partial(tables_kernel, pair_count, block_count),
        out_shape=jax.ShapeDtypeStruct((8, 2 * pairs), jnp.int32),
        in_specs=[smem, vmem, vmem],
        out_specs=vmem,
        compiler_params=limit,
        name="tables",
    )(place, pair_blocks, pair_live.reshape(1, pairs))
    state_index = lax.axis_index("state")
    quarter = node_features.shape[1]
    parts = weight_in.reshape(feat // quarter, quarter, hid)
    order = state_index ^ jnp.arange(feat // quarter)
    weights_here = jnp.take(parts, order, axis=0).reshape(feat, hid)
    other_split = swap(own_split, "state", 1)
    kept, sent = run_filter(
        places, blocks, slots, tables, own_split, other_split, weights_here,
        bias_in.reshape(1, hid), weights, pieces, fields,
    )
    return pl.pallas_call(
        finish_kernel,
        out_shape=[jax.ShapeDtypeStruct(states_in.shape, jnp.float32)] * 2,
        in_specs=[vmem] * 5,
        out_specs=[vmem, vmem],
        compiler_params=limit,
        name="finish",
    )(states_in, onsite_row, valid, kept, swap(sent, "state", 1))


def solution(mesh):
    return jax.shard_map(
        per_device,
        mesh=mesh,
        in_specs=(P("state", "pair"), P("pair"), P("pair", "state"), P(), P(), P(), P(), P(), P()),
        out_specs=(P("state", "pair"), P("state", "pair")),
        check_vma=False,
    )
```

```python
import functools

import jax
import jax.numpy as jnp
from jax import lax
from jax.experimental import pallas as pl
from jax.experimental.pallas import tpu as pltpu
from jax.sharding import PartitionSpec as P

ORB = 13
ATOM_BLK = 64
BO = ORB * ATOM_BLK
LANES = 128
PAD_ORB = 16
HALF = ATOM_BLK // 2
ROWS = HALF * PAD_ORB
COLS = ORB * LANES
WIDE = (ORB + 1) // 2 * LANES
STEP_ATOMS = 8
SLOT_GROUP = 8
TILE_BYTES = ROWS * COLS * 2
VMEM_LIMIT = 60 * 1024 * 1024
CACHE_BUDGET = 44 * 1024 * 1024


def dot(left, right):
    return jnp.dot(left, right, preferred_element_type=jnp.float32)


def dot_t(left, right):
    return lax.dot_general(left, right, (((1,), (1,)), ((), ())), preferred_element_type=jnp.float32)


def onehot_columns(rows, cols, row_of_col):
    col = lax.broadcasted_iota(jnp.int32, (1, cols), 1)
    row = lax.broadcasted_iota(jnp.int32, (rows, cols), 0)
    return jnp.where(row == row_of_col(col), 1.0, 0.0).astype(jnp.bfloat16)


def onehot_rows(rows, cols, col_of_row):
    row = lax.broadcasted_iota(jnp.int32, (rows, 1), 0)
    col = lax.broadcasted_iota(jnp.int32, (rows, cols), 1)
    return jnp.where(col == col_of_row(row), 1.0, 0.0).astype(jnp.bfloat16)


def natural_of_wide(lane):
    return jnp.where(lane < BO, lane % ATOM_BLK * ORB + lane // ATOM_BLK, -1)


def natural_of_split(parity, lane):
    orbital = lane % PAD_ORB
    return jnp.where(orbital < ORB, (lane // PAD_ORB * 2 + parity) * ORB + orbital, -1)


def wide_of_split(parity, lane):
    orbital = lane % PAD_ORB
    return jnp.where(orbital < ORB, orbital * ATOM_BLK + lane // PAD_ORB * 2 + parity, -1)


def natural_to_wide():
    return onehot_columns(BO, WIDE, natural_of_wide)


def natural_to_split(parity):
    return onehot_columns(BO, ROWS, functools.partial(natural_of_split, parity))


def split_to_natural(parity):
    return onehot_rows(ROWS, BO, functools.partial(natural_of_split, parity))


def split_to_wide(parity):
    return onehot_rows(ROWS, WIDE, functools.partial(wide_of_split, parity))


def as_row(column, eye):
    return jnp.sum(jnp.where(eye, column, 0), axis=0, keepdims=True)


def tables_kernel(pair_count, block_count, place_ref, blocks_ref, live_ref, tables_ref):
    me = place_ref[0]
    core = place_ref[1].astype(jnp.float32)
    pairs = blocks_ref.shape[0]
    ends = 2 * pairs
    blocks = pair_count * block_count
    eye = lax.broadcasted_iota(jnp.int32, (pairs, pairs), 0) == lax.broadcasted_iota(
        jnp.int32, (pairs, pairs), 1
    )
    firsts = as_row(blocks_ref[:, 0:1], eye)
    seconds = as_row(blocks_ref[:, 1:2], eye)
    target = jnp.concatenate([firsts, seconds], axis=1)
    source = jnp.concatenate([seconds, firsts], axis=1)
    live = jnp.concatenate([live_ref[...], live_ref[...]], axis=1) > 0
    lane = lax.broadcasted_iota(jnp.int32, (1, ends), 1)
    source_own = source // block_count == me
    own = live & (target // block_count == me)

    def number(flag):
        return jnp.where(flag, 1.0, 0.0)

    def whole(value):
        return value.astype(jnp.bfloat16)

    row = lax.broadcasted_iota(jnp.int32, (blocks, ends), 0)
    below = whole(
        number(
            lax.broadcasted_iota(jnp.int32, (blocks, blocks), 1)
            < lax.broadcasted_iota(jnp.int32, (blocks, blocks), 0)
        )
    )

    def before(column):
        return dot(below, whole(jnp.broadcast_to(column, (blocks, LANES))))[:, 0:1]

    def at(flag, column):
        return jnp.sum(jnp.where(flag, column, 0.0), axis=0, keepdims=True)

    is_source = row == source
    is_target = row == target
    own_ends = jnp.sum(number(is_source & own), axis=1, keepdims=True)
    has = number(own_ends > 0)
    following = live & (at(is_target, has) > 0) & jnp.logical_not(source_own)
    work = jnp.where(
        has > 0,
        3.0 * own_ends + 2.0 * jnp.sum(number(is_target & following), axis=1, keepdims=True),
        0.0,
    )
    work_total = jnp.sum(jnp.broadcast_to(work, (blocks, LANES)), axis=0, keepdims=True)[:, 0:1]
    half = number(2.0 * before(work) + work > work_total)
    mine = has * number(half == core)
    slot = before(mine)
    slot_total = jnp.sum(jnp.broadcast_to(mine, (blocks, LANES)), axis=0, keepdims=True)[:, 0:1]
    source_slot = at(is_source, slot)
    target_slot = at(is_target, slot)
    own = own & (at(is_source, mine) > 0)
    following = following & (at(is_target, mine) > 0)
    earlier = whole(
        number(
            lax.broadcasted_iota(jnp.int32, (ends, ends), 0)
            < lax.broadcasted_iota(jnp.int32, (ends, ends), 1)
        )
    )
    flags = jnp.concatenate(
        [number(own), number(following), jnp.zeros((6, ends), jnp.float32)], axis=0
    )
    ranks = dot(whole(flags), earlier)
    own_total = jnp.sum(number(own), axis=1, keepdims=True)
    total = own_total + jnp.sum(number(following), axis=1, keepdims=True)
    own_rank = jnp.where(own, ranks[0:1], -1.0)
    next_rank = jnp.where(following, own_total + ranks[1:2], -1.0)

    def position(block):
        return place_of((block // block_count) ^ me, pair_count) * block_count + block % block_count

    def fields(where, slots):
        rows = [
            position(target).astype(jnp.float32),
            position(source).astype(jnp.float32),
            number(lane >= pairs),
            where,
            slots,
        ]
        return whole(jnp.concatenate(rows + [jnp.zeros((3, ends), jnp.float32)], axis=0))

    spot = lax.broadcasted_iota(jnp.int32, (ends, ends), 0).astype(jnp.float32)
    placed = dot_t(
        fields((target % block_count).astype(jnp.float32), source_slot),
        whole(number(spot == own_rank)),
    ) + dot_t(fields(target_slot, target_slot), whole(number(spot == next_rank)))
    block_row = lax.broadcasted_iota(jnp.int32, (8, blocks), 1)
    slot_place = number(
        (lax.broadcasted_iota(jnp.int32, (blocks, ends), 1).astype(jnp.float32) == slot) & (mine > 0)
    )
    slot_block = dot(whole(position(block_row).astype(jnp.float32)), whole(slot_place))
    totals = jnp.where(
        lane == 0, own_total, jnp.where(lane == 1, total, jnp.where(lane == 2, slot_total, 0.0))
    )
    tables_ref[...] = jnp.concatenate(
        [placed[0:5], slot_block[0:1], totals, jnp.zeros((1, ends), jnp.float32)], axis=0
    ).astype(jnp.int32)


def prepare_kernel(
    block_count, states_ref, onsite_ref, valid_ref, payload_ref, own_split_ref, natural
):
    state_rows = states_ref.shape[0]
    extra = block_count * state_rows
    onsite_rows = []
    valid_rows = []
    for block in range(block_count):
        cut = slice(block * BO, (block + 1) * BO)
        valid = valid_ref[:, cut]
        natural[block * state_rows : (block + 1) * state_rows, :] = (
            states_ref[:, cut] * valid
        ).astype(jnp.bfloat16)
        onsite_rows.append(onsite_ref[:, cut] * valid)
        valid_rows.append(valid)
    natural[extra:, :] = jnp.concatenate(onsite_rows + valid_rows, axis=0).astype(jnp.bfloat16)
    payload_ref[...] = dot(natural[...], natural_to_wide()).astype(jnp.bfloat16)
    for parity in range(2):
        split = dot(natural[:extra, :], natural_to_split(parity)).astype(jnp.bfloat16)
        for block in range(block_count):
            own_split_ref[block, parity * state_rows : (parity + 1) * state_rows, :] = split[
                block * state_rows : (block + 1) * state_rows, :
            ]


def spread_states(fields):
    wide = fields.astype(jnp.float32)
    low = lax.broadcasted_iota(jnp.int32, (wide.shape[0], LANES), 1) < ATOM_BLK
    even, odd = [], []
    for column in range(WIDE // LANES):
        part = wide[:, column * LANES : (column + 1) * LANES]
        swapped = pltpu.roll(part, ATOM_BLK, 1)
        even += [jnp.where(low, part, 0.0), jnp.where(low, swapped, 0.0)]
        odd += [jnp.where(low, 0.0, swapped), jnp.where(low, 0.0, part)]
    return jnp.concatenate(
        [jnp.concatenate(even[:ORB], axis=1), jnp.concatenate(odd[:ORB], axis=1)], axis=0
    ).astype(jnp.bfloat16)


def fold_products(products):
    low = lax.broadcasted_iota(jnp.int32, (products.shape[0], LANES), 1) < ATOM_BLK
    sums = []
    for orbital in range(ORB):
        part = products[:, orbital * LANES : (orbital + 1) * LANES]
        sums.append(part + pltpu.roll(part, ATOM_BLK, 1))
    sums.append(jnp.zeros_like(sums[0]))
    return jnp.concatenate(
        [jnp.where(low, sums[2 * c], sums[2 * c + 1]) for c in range(WIDE // LANES)], axis=1
    )


def filter_kernel(
    cache, block_count, places, spots, tables_ref, bias_ref, own_split_hbm, other_split_hbm,
    weight_in_hbm, weight_out_hbm, *refs
):
    count = len(places)
    pieces = refs[:count]
    arrivals = refs[count:-19]
    (
        kept_ref, sent_ref, features_ref, fields_ref, feature_sems, field_sems,
        tiles, proj_target, proj_source, hidden, own_sums, again_sums, back_sums, next_sums, moved,
        split_ref, weight_in_ref, weight_out_ref, small_sems,
    ) = refs[-19:]
    state_rows = kept_ref.shape[1]
    small = [
        (own_split_hbm, split_ref.at[0]),
        (other_split_hbm, split_ref.at[1]),
        (weight_in_hbm, weight_in_ref),
        (weight_out_hbm, weight_out_ref),
    ]
    copies, late = [], []
    for index, (source, target) in enumerate(small):
        copies.append(pltpu.make_async_copy(source, target, small_sems.at[index]))
    for index, (piece, (start, rows, first, column)) in enumerate(zip(pieces, places)):
        copies.append(
            pltpu.make_async_copy(
                piece.at[start : start + rows],
                features_ref.at[first : first + rows, :, column : column + piece.shape[2]],
                feature_sems.at[index],
            )
        )
    for index, arrival in enumerate(arrivals):
        rows = slice(index % 2 * state_rows, (index % 2 + 1) * state_rows)
        for entry, spot in enumerate(spots[index // 2]):
            late.append(
                pltpu.make_async_copy(
                    arrival.at[entry], fields_ref.at[spot, :, rows], field_sems.at[index % 2, spot]
                )
            )
    for copy in copies + late:
        copy.start()
    own_total = tables_ref[6, 0]
    total = tables_ref[6, 1]
    both = 2 * state_rows
    slots = back_sums.shape[0]
    own_sums[...] = jnp.zeros_like(own_sums)
    again_sums[...] = jnp.zeros_like(again_sums)
    back_sums[...] = jnp.zeros_like(back_sums)
    next_sums[...] = jnp.zeros_like(next_sums)
    for copy in copies + late:
        copy.wait()

    def build_tile(task, keep):
        target = tables_ref[0, task]
        source = tables_ref[1, task]
        side = tables_ref[2, task]
        target_proj = dot(features_ref[target], weight_in_ref[...])
        proj_target[...] = (0.5 * (target_proj + bias_ref[...])).reshape(proj_target.shape)
        proj_source[...] = 0.5 * dot(features_ref[source], weight_in_ref[...])
        weight = weight_out_ref[side]

        def chunk(index, carry):
            targets = proj_target[index]
            for atom in range(STEP_ATOMS):
                half = targets[atom : atom + 1, :] + proj_source[...]
                hidden[atom * ATOM_BLK : (atom + 1) * ATOM_BLK, :] = (
                    half + half * jnp.tanh(half)
                ).astype(jnp.bfloat16)
            raw = dot_t(hidden[...], weight).astype(jnp.bfloat16).T
            for couple in range(STEP_ATOMS // 2):
                row = (index * (STEP_ATOMS // 2) + couple) * PAD_ORB
                for orbital in range(ORB):
                    tiles[
                        keep,
                        pl.ds(pl.multiple_of(row, PAD_ORB), PAD_ORB),
                        orbital * LANES : (orbital + 1) * LANES,
                    ] = raw[
                        orbital * PAD_ORB : (orbital + 1) * PAD_ORB,
                        couple * LANES : (couple + 1) * LANES,
                    ]
            return carry

        lax.fori_loop(0, ATOM_BLK // STEP_ATOMS, chunk, 0, unroll=True)

    def fields_of(block):
        return fields_ref[block // block_count, block % block_count]

    def first_pass(task, carry):
        keep = jnp.minimum(task, cache)
        build_tile(task, keep)
        where = tables_ref[3, task]
        spread = spread_states(fields_of(tables_ref[1, task]))
        arrived = dot_t(spread, tiles[keep])

        @pl.when(task < own_total)
        def _():
            own_sums[where] += arrived
            fields = jnp.concatenate(
                [
                    split_ref[core, where, parity * state_rows : (parity + 1) * state_rows]
                    for parity in range(2)
                    for core in range(2)
                ],
                axis=0,
            )
            back = dot(fields, tiles[keep])
            low = lax.broadcasted_iota(jnp.int32, (both, COLS), 1) % LANES < ATOM_BLK
            back_sums[tables_ref[4, task]] += jnp.where(low, back[:both], back[both:])

        @pl.when(task >= own_total)
        def _():
            next_sums[where] += arrived

        return carry

    lax.fori_loop(0, total, first_pass, 0)


    def to_layout(sums, matrix):
        groups = sums.shape[0]
        result = 0.0
        for parity in range(2):
            rows = sums[:, parity * both : (parity + 1) * both, :]
            rows = rows.reshape(groups * both, ROWS).astype(jnp.bfloat16)
            result = result + dot(rows, matrix(parity))
        return result

    def put(step, sums):
        natural = to_layout(sums, split_to_natural)
        for block in range(block_count):
            cut = slice(block * BO, (block + 1) * BO)
            middle = block * both + state_rows
            kept_ref[step, :, cut] = natural[block * both : middle]
            sent_ref[step, :, cut] = natural[middle : (block + 1) * both].astype(jnp.bfloat16)

    put(0, own_sums[...])
    for start in range(0, slots, SLOT_GROUP):

        @pl.when(start < tables_ref[6, 2])
        def _():
            moved_next = to_layout(next_sums[start : start + SLOT_GROUP], split_to_wide)
            for slot in range(start, min(start + SLOT_GROUP, slots)):
                block = tables_ref[5, slot]
                owner = block // block_count
                local = block % block_count
                extras = fields_ref[owner, block_count, :state_rows].astype(jnp.float32)
                row = lax.broadcasted_iota(jnp.int32, extras.shape, 0)
                onsite = jnp.sum(jnp.where(row == local, extras, 0.0), axis=0, keepdims=True)
                valid = jnp.sum(
                    jnp.where(row == local + block_count, extras, 0.0), axis=0, keepdims=True
                )
                part = (slot - start) * both
                products = moved_next[part : part + both] + fold_products(back_sums[slot])
                moved[slot] = (
                    fields_ref[owner, local].astype(jnp.float32) * onsite + products * valid
                ).astype(jnp.bfloat16)

    def second_pass(task, carry):
        keep = jnp.minimum(task, cache)

        @pl.when(task >= cache)
        def _():
            build_tile(task, keep)

        slot = tables_ref[4, task]
        again_sums[tables_ref[3, task]] += dot_t(spread_states(moved[slot]), tiles[keep])
        return carry

    lax.fori_loop(0, own_total, second_pass, 0)
    put(1, again_sums[...])


def finish_kernel(states_ref, onsite_ref, valid_ref, kept_ref, got_ref, first_ref, second_ref):
    states = states_ref[...]
    onsite = onsite_ref[...]
    valid = valid_ref[...]
    first = states * onsite + (kept_ref[0] + got_ref[0].astype(jnp.float32)) * valid
    first_ref[...] = first
    again = (kept_ref[1] + got_ref[1].astype(jnp.float32)) * valid
    second_ref[...] = 2.0 * (first * onsite + again) - states


def swap(value, axis, offset):
    size = lax.axis_size(axis)
    return lax.ppermute(value, axis, [(index, index ^ offset) for index in range(size)])


def place_of(offset, size):
    half = size // 2
    within = offset % half
    return offset // half * half + within % 2 * (half // 2) + within // 2


def after(value, *earlier):
    return lax.optimization_barrier((value, *earlier))[0]


def far_entries(value):
    entries = {0: value}
    bit = lax.axis_size("pair") // 2
    while bit > 1:
        entries.update({old ^ bit: swap(entry, "pair", bit) for old, entry in entries.items()})
        bit //= 2
    return entries


def gather_features(features):
    far = far_entries(features)
    return far, swap(features, "pair", 1)


def spread_features(far, near):
    atoms, quarter = far[0].shape
    pieces, places = [], []
    offsets = sorted(far)
    middle = len(offsets) // 2
    first_row = 0
    for start, group in ((0, offsets[:middle]), (middle, offsets[middle:])):
        if start == 0:
            besides = [near] + [swap(far[offset], "pair", 1) for offset in group[1:]]
            both = jnp.concatenate([far[offset] for offset in group] + besides, axis=0)
        else:
            late = jnp.concatenate([far[offset] for offset in group], axis=0)
            both = jnp.concatenate([late, swap(late, "pair", 1)], axis=0)
        bundle = [both]
        for part in range(2, lax.axis_size("state"), 2):
            bundle.append(swap(both, "state", part))
        rows = both.shape[0]
        bundle = jnp.concatenate(bundle, axis=0)
        if start == 0:
            first_bundle = bundle
        other = swap(bundle, "state", 1)
        for part in range(bundle.shape[0] // rows):
            cut = slice(part * rows, (part + 1) * rows)
            couple = [(bundle, part * rows), (other, part * rows)]
            if quarter % LANES:
                couple = [(jnp.concatenate([bundle[cut], other[cut]], axis=1), 0)]
            for side, (piece, begin) in enumerate(couple):
                pieces.append(piece)
                places.append((begin, rows, first_row, (2 * part + side) * quarter))
        first_row += rows
    return pieces, places, first_bundle


def gather_fields(payload, ready):
    far = far_entries(payload)
    last = max(far)
    far[last] = after(far[last], *ready)
    fields, spots = [], []
    offsets = sorted(far)
    for group in (offsets[:2], offsets[2:]):
        bundle = jnp.stack([far[offset] for offset in group])
        fields.append(jnp.concatenate([bundle, swap(bundle, "pair", 1)], axis=0))
        spots.append([place_of(offset, lax.axis_size("pair")) for offset in group] + [place_of(offset + 1, lax.axis_size("pair")) for offset in group])
    return fields, spots


def run_filter(
    places, spots, blocks, slots, tables, own_split, other_split, weights_here, bias_row, weights,
    pieces, fields,
):
    feat, hid = weights_here.shape
    pair_count = sum(len(entries) for entries in spots)
    _, groups, state_rows, _ = fields[0].shape
    block_count = blocks // pair_count
    both = 2 * state_rows
    held = blocks * ATOM_BLK * feat * 2 + 2 * pair_count * fields[0][0].size * 2
    held += slots * both * (COLS + 2 * ROWS) * 4
    cache = max(1, min(slots, (CACHE_BUDGET - held) // TILE_BYTES))
    smem = pl.BlockSpec(memory_space=pltpu.SMEM)
    vmem = pl.BlockSpec(memory_space=pltpu.VMEM)
    hbm = pl.BlockSpec(memory_space=pl.ANY)
    partial = (2, state_rows, block_count * BO)
    return pl.pallas_call(
        functools.partial(filter_kernel, cache, block_count, places, spots),
        out_shape=[
            jax.ShapeDtypeStruct(partial, jnp.float32),
            jax.ShapeDtypeStruct(partial, jnp.bfloat16),
        ],
        in_specs=[smem, vmem] + [hbm] * (4 + len(pieces) + len(fields)),
        out_specs=[vmem, vmem],
        scratch_shapes=[
            pltpu.VMEM((blocks, ATOM_BLK, feat), jnp.bfloat16),
            pltpu.VMEM((pair_count, groups, both, WIDE), jnp.bfloat16),
            pltpu.SemaphoreType.DMA((len(pieces),)),
            pltpu.SemaphoreType.DMA((2, pair_count)),
            pltpu.VMEM((cache + 1, ROWS, COLS), jnp.bfloat16),
            pltpu.VMEM((ATOM_BLK // STEP_ATOMS, STEP_ATOMS, hid), jnp.float32),
            pltpu.VMEM((ATOM_BLK, hid), jnp.float32),
            pltpu.VMEM((STEP_ATOMS * ATOM_BLK, hid), jnp.bfloat16),
            pltpu.VMEM((block_count, 2 * both, ROWS), jnp.float32),
            pltpu.VMEM((block_count, 2 * both, ROWS), jnp.float32),
            pltpu.VMEM((slots, both, COLS), jnp.float32),
            pltpu.VMEM((slots, 2 * both, ROWS), jnp.float32),
            pltpu.VMEM((slots, both, WIDE), jnp.bfloat16),
            pltpu.VMEM((2,) + own_split.shape, jnp.bfloat16),
            pltpu.VMEM(weights_here.shape, jnp.bfloat16),
            pltpu.VMEM(weights.shape, jnp.bfloat16),
            pltpu.SemaphoreType.DMA((4,)),
        ],
        compiler_params=pltpu.CompilerParams(vmem_limit_bytes=VMEM_LIMIT),
        name="filter",
    )(
        tables, bias_row, own_split, other_split, weights_here, weights, *pieces, *fields,
    )


def per_device(
    states_in, onsite, node_features, atom_orbitals, pair_blocks, pair_live, weight_in, bias_in,
    weight_out,
):
    pair_count = lax.axis_size("pair")
    state_rows = states_in.shape[0]
    block_count = onsite.shape[0] // BO
    blocks = pair_count * block_count
    pairs = pair_live.shape[0]
    pairs_here = pairs // pair_count
    end_count = 2 * pairs_here
    slots = pair_count * ((end_count + pair_count - 1) // pair_count)
    hid = weight_in.shape[1]
    feat = weight_in.shape[0]
    far, near = gather_features(node_features)
    place = jnp.stack([lax.axis_index("pair"), lax.axis_index("state") % 2]).astype(jnp.int32)
    atoms_here = node_features.shape[0]
    own_orbitals = lax.dynamic_slice_in_dim(atom_orbitals, place[0] * atoms_here, atoms_here)
    valid = (jnp.arange(ORB)[None, :] < own_orbitals[:, None]).astype(jnp.float32)
    valid = valid.reshape(1, atoms_here * ORB)
    onsite_row = onsite.reshape(1, -1)
    smem = pl.BlockSpec(memory_space=pltpu.SMEM)
    vmem = pl.BlockSpec(memory_space=pltpu.VMEM)
    hbm = pl.BlockSpec(memory_space=pl.ANY)
    groups = block_count + (2 * block_count + state_rows - 1) // state_rows
    limit = pltpu.CompilerParams(vmem_limit_bytes=VMEM_LIMIT)
    payload, own_split = pl.pallas_call(
        functools.partial(prepare_kernel, block_count),
        out_shape=[
            jax.ShapeDtypeStruct((groups * state_rows, WIDE), jnp.bfloat16),
            jax.ShapeDtypeStruct((block_count, 2 * state_rows, ROWS), jnp.bfloat16),
        ],
        in_specs=[vmem, vmem, vmem],
        out_specs=[vmem, vmem],
        scratch_shapes=[pltpu.VMEM((groups * state_rows, BO), jnp.bfloat16)],
        compiler_params=limit,
        name="prepare",
    )(states_in, onsite_row, valid)
    payload = after(payload, *[far[offset] for offset in sorted(far)[1:]])
    pieces, places, bundle = spread_features(far, near)
    pair_blocks, weight_in, weight_out = after(
        (pair_blocks, weight_in, weight_out), far[max(far)]
    )
    pieces = [piece.reshape(-1, ATOM_BLK, piece.shape[1]) for piece in pieces]
    places = [
        (start // ATOM_BLK, rows // ATOM_BLK, first // ATOM_BLK, column)
        for start, rows, first, column in places
    ]
    cube = weight_out.reshape(hid, ORB, ORB).astype(jnp.float32)
    pad = ((0, 0), (0, PAD_ORB - ORB), (0, 0))
    weights = jnp.stack(
        [
            jnp.pad(cube.transpose(2, 1, 0), pad).reshape(ORB * PAD_ORB, hid),
            jnp.pad(cube.transpose(1, 2, 0), pad).reshape(ORB * PAD_ORB, hid),
        ]
    ).astype(jnp.bfloat16)

    tables = pl.pallas_call(
        functools.partial(tables_kernel, pair_count, block_count),
        out_shape=jax.ShapeDtypeStruct((8, 2 * pairs), jnp.int32),
        in_specs=[smem, vmem, vmem],
        out_specs=vmem,
        compiler_params=limit,
        name="tables",
    )(place, pair_blocks, pair_live.reshape(1, pairs))
    state_index = lax.axis_index("state")
    quarter = node_features.shape[1]
    parts = weight_in.reshape(feat // quarter, quarter, hid)
    order = state_index ^ jnp.arange(feat // quarter)
    weights_here = jnp.take(parts, order, axis=0).reshape(feat, hid)
    other_split = swap(own_split, "state", 1)
    own_fields, spots = gather_fields(
        payload.reshape(groups, state_rows, WIDE), (tables, weights_here, weights, other_split)
    )
    fields = []
    for entry in own_fields:
        fields += [entry, swap(entry, "state", 1)]
    kept, sent = run_filter(
        places, spots, blocks, slots, tables, own_split, other_split, weights_here,
        bias_in.reshape(1, hid), weights, pieces, fields,
    )
    return pl.pallas_call(
        finish_kernel,
        out_shape=[jax.ShapeDtypeStruct(states_in.shape, jnp.float32)] * 2,
        in_specs=[vmem] * 5,
        out_specs=[vmem, vmem],
        compiler_params=limit,
        name="finish",
    )(states_in, onsite_row, valid, kept, swap(sent, "state", 1))


def solution(mesh):
    return jax.shard_map(
        per_device,
        mesh=mesh,
        in_specs=(P("state", "pair"), P("pair"), P("pair", "state"), P(), P(), P(), P(), P(), P()),
        out_specs=(P("state", "pair"), P("state", "pair")),
        check_vma=False,
    )
```

```python
import functools

import jax
import jax.numpy as jnp
from jax import lax
from jax.experimental import pallas as pl
from jax.experimental.pallas import tpu as pltpu
from jax.sharding import PartitionSpec as P

ORB = 13
ATOM_BLK = 64
BO = ORB * ATOM_BLK
LANES = 128
PAD_ORB = 16
HALF = ATOM_BLK // 2
ROWS = HALF * PAD_ORB
COLS = ORB * LANES
WIDE = (ORB + 1) // 2 * LANES
STEP_ATOMS = 8
SLOT_GROUP = 8
TILE_BYTES = ROWS * COLS * 2
VMEM_LIMIT = 60 * 1024 * 1024
CACHE_BUDGET = 44 * 1024 * 1024


def dot(left, right):
    return jnp.dot(left, right, preferred_element_type=jnp.float32)


def dot_t(left, right):
    return lax.dot_general(left, right, (((1,), (1,)), ((), ())), preferred_element_type=jnp.float32)


def onehot_columns(rows, cols, row_of_col):
    col = lax.broadcasted_iota(jnp.int32, (1, cols), 1)
    row = lax.broadcasted_iota(jnp.int32, (rows, cols), 0)
    return jnp.where(row == row_of_col(col), 1.0, 0.0).astype(jnp.bfloat16)


def onehot_rows(rows, cols, col_of_row):
    row = lax.broadcasted_iota(jnp.int32, (rows, 1), 0)
    col = lax.broadcasted_iota(jnp.int32, (rows, cols), 1)
    return jnp.where(col == col_of_row(row), 1.0, 0.0).astype(jnp.bfloat16)


def natural_of_wide(lane):
    return jnp.where(lane < BO, lane % ATOM_BLK * ORB + lane // ATOM_BLK, -1)


def natural_of_split(parity, lane):
    orbital = lane % PAD_ORB
    return jnp.where(orbital < ORB, (lane // PAD_ORB * 2 + parity) * ORB + orbital, -1)


def wide_of_split(parity, lane):
    orbital = lane % PAD_ORB
    return jnp.where(orbital < ORB, orbital * ATOM_BLK + lane // PAD_ORB * 2 + parity, -1)


def natural_to_wide():
    return onehot_columns(BO, WIDE, natural_of_wide)


def natural_to_split(parity):
    return onehot_columns(BO, ROWS, functools.partial(natural_of_split, parity))


def split_to_natural(parity):
    return onehot_rows(ROWS, BO, functools.partial(natural_of_split, parity))


def split_to_wide(parity):
    return onehot_rows(ROWS, WIDE, functools.partial(wide_of_split, parity))


def as_row(column, eye):
    return jnp.sum(jnp.where(eye, column, 0), axis=0, keepdims=True)


def tables_kernel(pair_count, block_count, place_ref, blocks_ref, live_ref, tables_ref):
    me = place_ref[0]
    core = place_ref[1].astype(jnp.float32)
    pairs = blocks_ref.shape[0]
    ends = 2 * pairs
    blocks = pair_count * block_count
    eye = lax.broadcasted_iota(jnp.int32, (pairs, pairs), 0) == lax.broadcasted_iota(
        jnp.int32, (pairs, pairs), 1
    )
    firsts = as_row(blocks_ref[:, 0:1], eye)
    seconds = as_row(blocks_ref[:, 1:2], eye)
    target = jnp.concatenate([firsts, seconds], axis=1)
    source = jnp.concatenate([seconds, firsts], axis=1)
    live = jnp.concatenate([live_ref[...], live_ref[...]], axis=1) > 0
    lane = lax.broadcasted_iota(jnp.int32, (1, ends), 1)
    source_own = source // block_count == me
    own = live & (target // block_count == me)

    def number(flag):
        return jnp.where(flag, 1.0, 0.0)

    def whole(value):
        return value.astype(jnp.bfloat16)

    row = lax.broadcasted_iota(jnp.int32, (blocks, ends), 0)
    below = whole(
        number(
            lax.broadcasted_iota(jnp.int32, (blocks, blocks), 1)
            < lax.broadcasted_iota(jnp.int32, (blocks, blocks), 0)
        )
    )

    def before(column):
        return dot(below, whole(jnp.broadcast_to(column, (blocks, LANES))))[:, 0:1]

    def at(flag, column):
        return jnp.sum(jnp.where(flag, column, 0.0), axis=0, keepdims=True)

    is_source = row == source
    is_target = row == target
    own_ends = jnp.sum(number(is_source & own), axis=1, keepdims=True)
    has = number(own_ends > 0)
    following = live & (at(is_target, has) > 0) & jnp.logical_not(source_own)
    work = jnp.where(
        has > 0,
        3.0 * own_ends + 2.0 * jnp.sum(number(is_target & following), axis=1, keepdims=True),
        0.0,
    )
    work_total = jnp.sum(jnp.broadcast_to(work, (blocks, LANES)), axis=0, keepdims=True)[:, 0:1]
    half = number(2.0 * before(work) + work > work_total)
    mine = has * number(half == core)
    slot = before(mine)
    slot_total = jnp.sum(jnp.broadcast_to(mine, (blocks, LANES)), axis=0, keepdims=True)[:, 0:1]
    source_slot = at(is_source, slot)
    target_slot = at(is_target, slot)
    own = own & (at(is_source, mine) > 0)
    following = following & (at(is_target, mine) > 0)
    earlier = whole(
        number(
            lax.broadcasted_iota(jnp.int32, (ends, ends), 0)
            < lax.broadcasted_iota(jnp.int32, (ends, ends), 1)
        )
    )
    flags = jnp.concatenate(
        [number(own), number(following), jnp.zeros((6, ends), jnp.float32)], axis=0
    )
    ranks = dot(whole(flags), earlier)
    own_total = jnp.sum(number(own), axis=1, keepdims=True)
    total = own_total + jnp.sum(number(following), axis=1, keepdims=True)
    own_rank = jnp.where(own, ranks[0:1], -1.0)
    next_rank = jnp.where(following, own_total + ranks[1:2], -1.0)

    def position(block):
        return place_of((block // block_count) ^ me, pair_count) * block_count + block % block_count

    def fields(where, slots):
        rows = [
            position(target).astype(jnp.float32),
            position(source).astype(jnp.float32),
            number(lane >= pairs),
            where,
            slots,
        ]
        return whole(jnp.concatenate(rows + [jnp.zeros((3, ends), jnp.float32)], axis=0))

    spot = lax.broadcasted_iota(jnp.int32, (ends, ends), 0).astype(jnp.float32)
    placed = dot_t(
        fields((target % block_count).astype(jnp.float32), source_slot),
        whole(number(spot == own_rank)),
    ) + dot_t(fields(target_slot, target_slot), whole(number(spot == next_rank)))
    block_row = lax.broadcasted_iota(jnp.int32, (8, blocks), 1)
    slot_place = number(
        (lax.broadcasted_iota(jnp.int32, (blocks, ends), 1).astype(jnp.float32) == slot) & (mine > 0)
    )
    slot_block = dot(whole(position(block_row).astype(jnp.float32)), whole(slot_place))
    totals = jnp.where(
        lane == 0, own_total, jnp.where(lane == 1, total, jnp.where(lane == 2, slot_total, 0.0))
    )
    tables_ref[...] = jnp.concatenate(
        [placed[0:5], slot_block[0:1], totals, jnp.zeros((1, ends), jnp.float32)], axis=0
    ).astype(jnp.int32)


def prepare_kernel(
    block_count, states_ref, onsite_ref, valid_ref, payload_ref, own_split_ref, natural
):
    state_rows = states_ref.shape[0]
    extra = block_count * state_rows
    onsite_rows = []
    valid_rows = []
    for block in range(block_count):
        cut = slice(block * BO, (block + 1) * BO)
        valid = valid_ref[:, cut]
        natural[block * state_rows : (block + 1) * state_rows, :] = (
            states_ref[:, cut] * valid
        ).astype(jnp.bfloat16)
        onsite_rows.append(onsite_ref[:, cut] * valid)
        valid_rows.append(valid)
    natural[extra:, :] = jnp.concatenate(onsite_rows + valid_rows, axis=0).astype(jnp.bfloat16)
    payload_ref[...] = dot(natural[...], natural_to_wide()).astype(jnp.bfloat16)
    for parity in range(2):
        split = dot(natural[:extra, :], natural_to_split(parity)).astype(jnp.bfloat16)
        for block in range(block_count):
            own_split_ref[block, parity * state_rows : (parity + 1) * state_rows, :] = split[
                block * state_rows : (block + 1) * state_rows, :
            ]


def spread_states(fields):
    wide = fields.astype(jnp.float32)
    low = lax.broadcasted_iota(jnp.int32, (wide.shape[0], LANES), 1) < ATOM_BLK
    even, odd = [], []
    for column in range(WIDE // LANES):
        part = wide[:, column * LANES : (column + 1) * LANES]
        swapped = pltpu.roll(part, ATOM_BLK, 1)
        even += [jnp.where(low, part, 0.0), jnp.where(low, swapped, 0.0)]
        odd += [jnp.where(low, 0.0, swapped), jnp.where(low, 0.0, part)]
    return jnp.concatenate(
        [jnp.concatenate(even[:ORB], axis=1), jnp.concatenate(odd[:ORB], axis=1)], axis=0
    ).astype(jnp.bfloat16)


def fold_products(products):
    low = lax.broadcasted_iota(jnp.int32, (products.shape[0], LANES), 1) < ATOM_BLK
    sums = []
    for orbital in range(ORB):
        part = products[:, orbital * LANES : (orbital + 1) * LANES]
        sums.append(part + pltpu.roll(part, ATOM_BLK, 1))
    sums.append(jnp.zeros_like(sums[0]))
    return jnp.concatenate(
        [jnp.where(low, sums[2 * c], sums[2 * c + 1]) for c in range(WIDE // LANES)], axis=1
    )


def filter_kernel(
    cache, block_count, places, spots, tables_ref, bias_ref, own_split_hbm, other_split_hbm,
    weight_in_hbm, weight_out_hbm, *refs
):
    count = len(places)
    pieces = refs[:count]
    arrivals = refs[count:-19]
    (
        kept_ref, sent_ref, features_ref, fields_ref, feature_sems, field_sems,
        tiles, proj_target, proj_source, hidden, own_sums, again_sums, back_sums, next_sums, moved,
        split_ref, weight_in_ref, weight_out_ref, small_sems,
    ) = refs[-19:]
    state_rows = kept_ref.shape[1]
    small = [
        (own_split_hbm, split_ref.at[0]),
        (other_split_hbm, split_ref.at[1]),
        (weight_in_hbm, weight_in_ref),
        (weight_out_hbm, weight_out_ref),
    ]
    copies, late = [], []
    for index, (source, target) in enumerate(small):
        copies.append(pltpu.make_async_copy(source, target, small_sems.at[index]))
    for index, (piece, (start, rows, first, column)) in enumerate(zip(pieces, places)):
        copies.append(
            pltpu.make_async_copy(
                piece.at[start : start + rows],
                features_ref.at[first : first + rows, :, column : column + piece.shape[2]],
                feature_sems.at[index],
            )
        )
    for index, arrival in enumerate(arrivals):
        rows = slice(index % 2 * state_rows, (index % 2 + 1) * state_rows)
        for entry, spot in enumerate(spots[index // 2]):
            late.append(
                pltpu.make_async_copy(
                    arrival.at[entry], fields_ref.at[spot, :, rows], field_sems.at[index % 2, spot]
                )
            )
    for copy in copies + late:
        copy.start()
    own_total = tables_ref[6, 0]
    total = tables_ref[6, 1]
    both = 2 * state_rows
    slots = back_sums.shape[0]
    own_sums[...] = jnp.zeros_like(own_sums)
    again_sums[...] = jnp.zeros_like(again_sums)
    back_sums[...] = jnp.zeros_like(back_sums)
    next_sums[...] = jnp.zeros_like(next_sums)
    for copy in copies + late:
        copy.wait()

    def build_tile(task, keep):
        target = tables_ref[0, task]
        source = tables_ref[1, task]
        side = tables_ref[2, task]
        target_proj = dot(features_ref[target], weight_in_ref[...])
        proj_target[...] = (0.5 * (target_proj + bias_ref[...])).reshape(proj_target.shape)
        proj_source[...] = 0.5 * dot(features_ref[source], weight_in_ref[...])
        weight = weight_out_ref[side]

        def chunk(index, carry):
            targets = proj_target[index]
            for atom in range(STEP_ATOMS):
                half = targets[atom : atom + 1, :] + proj_source[...]
                hidden[atom * ATOM_BLK : (atom + 1) * ATOM_BLK, :] = (
                    half + half * jnp.tanh(half)
                ).astype(jnp.bfloat16)
            raw = dot_t(hidden[...], weight).astype(jnp.bfloat16).T
            for couple in range(STEP_ATOMS // 2):
                row = (index * (STEP_ATOMS // 2) + couple) * PAD_ORB
                for orbital in range(ORB):
                    tiles[
                        keep,
                        pl.ds(pl.multiple_of(row, PAD_ORB), PAD_ORB),
                        orbital * LANES : (orbital + 1) * LANES,
                    ] = raw[
                        orbital * PAD_ORB : (orbital + 1) * PAD_ORB,
                        couple * LANES : (couple + 1) * LANES,
                    ]
            return carry

        lax.fori_loop(0, ATOM_BLK // STEP_ATOMS, chunk, 0, unroll=True)

    def fields_of(block):
        return fields_ref[block // block_count, block % block_count]

    def first_pass(task, carry):
        keep = jnp.minimum(task, cache)
        build_tile(task, keep)
        where = tables_ref[3, task]
        spread = spread_states(fields_of(tables_ref[1, task]))
        arrived = dot_t(spread, tiles[keep])

        @pl.when(task < own_total)
        def _():
            own_sums[where] += arrived
            fields = jnp.concatenate(
                [
                    split_ref[core, where, parity * state_rows : (parity + 1) * state_rows]
                    for parity in range(2)
                    for core in range(2)
                ],
                axis=0,
            )
            back = dot(fields, tiles[keep])
            low = lax.broadcasted_iota(jnp.int32, (both, COLS), 1) % LANES < ATOM_BLK
            back_sums[tables_ref[4, task]] += jnp.where(low, back[:both], back[both:])

        @pl.when(task >= own_total)
        def _():
            next_sums[where] += arrived

        return carry

    lax.fori_loop(0, total, first_pass, 0)


    def to_layout(sums, matrix):
        groups = sums.shape[0]
        result = 0.0
        for parity in range(2):
            rows = sums[:, parity * both : (parity + 1) * both, :]
            rows = rows.reshape(groups * both, ROWS).astype(jnp.bfloat16)
            result = result + dot(rows, matrix(parity))
        return result

    def put(step, sums):
        natural = to_layout(sums, split_to_natural)
        for block in range(block_count):
            cut = slice(block * BO, (block + 1) * BO)
            middle = block * both + state_rows
            kept_ref[step, :, cut] = natural[block * both : middle]
            sent_ref[step, :, cut] = natural[middle : (block + 1) * both].astype(jnp.bfloat16)

    put(0, own_sums[...])
    for start in range(0, slots, SLOT_GROUP):

        @pl.when(start < tables_ref[6, 2])
        def _():
            moved_next = to_layout(next_sums[start : start + SLOT_GROUP], split_to_wide)
            for slot in range(start, min(start + SLOT_GROUP, slots)):
                block = tables_ref[5, slot]
                owner = block // block_count
                local = block % block_count
                extras = fields_ref[owner, block_count, :state_rows].astype(jnp.float32)
                row = lax.broadcasted_iota(jnp.int32, extras.shape, 0)
                onsite = jnp.sum(jnp.where(row == local, extras, 0.0), axis=0, keepdims=True)
                valid = jnp.sum(
                    jnp.where(row == local + block_count, extras, 0.0), axis=0, keepdims=True
                )
                part = (slot - start) * both
                products = moved_next[part : part + both] + fold_products(back_sums[slot])
                moved[slot] = (
                    fields_ref[owner, local].astype(jnp.float32) * onsite + products * valid
                ).astype(jnp.bfloat16)

    def second_pass(task, carry):
        keep = jnp.minimum(task, cache)

        @pl.when(task >= cache)
        def _():
            build_tile(task, keep)

        slot = tables_ref[4, task]
        again_sums[tables_ref[3, task]] += dot_t(spread_states(moved[slot]), tiles[keep])
        return carry

    lax.fori_loop(0, own_total, second_pass, 0)
    put(1, again_sums[...])


def swap(value, axis, offset):
    size = lax.axis_size(axis)
    return lax.ppermute(value, axis, [(index, index ^ offset) for index in range(size)])


def place_of(offset, size):
    half = size // 2
    within = offset % half
    return offset // half * half + within % 2 * (half // 2) + within // 2


def after(value, *earlier):
    return lax.optimization_barrier((value, *earlier))[0]


def far_entries(value):
    entries = {0: value}
    bit = lax.axis_size("pair") // 2
    while bit > 1:
        entries.update({old ^ bit: swap(entry, "pair", bit) for old, entry in entries.items()})
        bit //= 2
    return entries


def gather_features(features):
    far = far_entries(features)
    return far, swap(features, "pair", 1)


def spread_features(far, near):
    atoms, quarter = far[0].shape
    pieces, places = [], []
    offsets = sorted(far)
    middle = len(offsets) // 2
    first_row = 0
    for start, group in ((0, offsets[:middle]), (middle, offsets[middle:])):
        if start == 0:
            besides = [near] + [swap(far[offset], "pair", 1) for offset in group[1:]]
            both = jnp.concatenate([far[offset] for offset in group] + besides, axis=0)
        else:
            late = jnp.concatenate([far[offset] for offset in group], axis=0)
            both = jnp.concatenate([late, swap(late, "pair", 1)], axis=0)
        bundle = [both]
        for part in range(2, lax.axis_size("state"), 2):
            bundle.append(swap(both, "state", part))
        rows = both.shape[0]
        bundle = jnp.concatenate(bundle, axis=0)
        if start == 0:
            first_bundle = bundle
        other = swap(bundle, "state", 1)
        for part in range(bundle.shape[0] // rows):
            cut = slice(part * rows, (part + 1) * rows)
            couple = [(bundle, part * rows), (other, part * rows)]
            if quarter % LANES:
                couple = [(jnp.concatenate([bundle[cut], other[cut]], axis=1), 0)]
            for side, (piece, begin) in enumerate(couple):
                pieces.append(piece)
                places.append((begin, rows, first_row, (2 * part + side) * quarter))
        first_row += rows
    return pieces, places, first_bundle


def gather_fields(payload, ready):
    far = far_entries(payload)
    last = max(far)
    far[last] = after(far[last], *ready)
    fields, spots = [], []
    offsets = sorted(far)
    for group in (offsets[:2], offsets[2:]):
        bundle = jnp.stack([far[offset] for offset in group])
        fields.append(jnp.concatenate([bundle, swap(bundle, "pair", 1)], axis=0))
        spots.append([place_of(offset, lax.axis_size("pair")) for offset in group] + [place_of(offset + 1, lax.axis_size("pair")) for offset in group])
    return fields, spots


def run_filter(
    places, spots, blocks, slots, tables, own_split, other_split, weights_here, bias_row, weights,
    pieces, fields,
):
    feat, hid = weights_here.shape
    pair_count = sum(len(entries) for entries in spots)
    _, groups, state_rows, _ = fields[0].shape
    block_count = blocks // pair_count
    both = 2 * state_rows
    held = blocks * ATOM_BLK * feat * 2 + 2 * pair_count * fields[0][0].size * 2
    held += slots * both * (COLS + 2 * ROWS) * 4
    cache = max(1, min(slots, (CACHE_BUDGET - held) // TILE_BYTES))
    smem = pl.BlockSpec(memory_space=pltpu.SMEM)
    vmem = pl.BlockSpec(memory_space=pltpu.VMEM)
    hbm = pl.BlockSpec(memory_space=pl.ANY)
    partial = (2, state_rows, block_count * BO)
    return pl.pallas_call(
        functools.partial(filter_kernel, cache, block_count, places, spots),
        out_shape=[
            jax.ShapeDtypeStruct(partial, jnp.float32),
            jax.ShapeDtypeStruct(partial, jnp.bfloat16),
        ],
        in_specs=[smem, vmem] + [hbm] * (4 + len(pieces) + len(fields)),
        out_specs=[vmem, vmem],
        scratch_shapes=[
            pltpu.VMEM((blocks, ATOM_BLK, feat), jnp.bfloat16),
            pltpu.VMEM((pair_count, groups, both, WIDE), jnp.bfloat16),
            pltpu.SemaphoreType.DMA((len(pieces),)),
            pltpu.SemaphoreType.DMA((2, pair_count)),
            pltpu.VMEM((cache + 1, ROWS, COLS), jnp.bfloat16),
            pltpu.VMEM((ATOM_BLK // STEP_ATOMS, STEP_ATOMS, hid), jnp.float32),
            pltpu.VMEM((ATOM_BLK, hid), jnp.float32),
            pltpu.VMEM((STEP_ATOMS * ATOM_BLK, hid), jnp.bfloat16),
            pltpu.VMEM((block_count, 2 * both, ROWS), jnp.float32),
            pltpu.VMEM((block_count, 2 * both, ROWS), jnp.float32),
            pltpu.VMEM((slots, both, COLS), jnp.float32),
            pltpu.VMEM((slots, 2 * both, ROWS), jnp.float32),
            pltpu.VMEM((slots, both, WIDE), jnp.bfloat16),
            pltpu.VMEM((2,) + own_split.shape, jnp.bfloat16),
            pltpu.VMEM(weights_here.shape, jnp.bfloat16),
            pltpu.VMEM(weights.shape, jnp.bfloat16),
            pltpu.SemaphoreType.DMA((4,)),
        ],
        compiler_params=pltpu.CompilerParams(vmem_limit_bytes=VMEM_LIMIT),
        name="filter",
    )(
        tables, bias_row, own_split, other_split, weights_here, weights, *pieces, *fields,
    )


def per_device(
    states_in, onsite, node_features, atom_orbitals, pair_blocks, pair_live, weight_in, bias_in,
    weight_out,
):
    pair_count = lax.axis_size("pair")
    state_rows = states_in.shape[0]
    block_count = onsite.shape[0] // BO
    blocks = pair_count * block_count
    pairs = pair_live.shape[0]
    pairs_here = pairs // pair_count
    end_count = 2 * pairs_here
    slots = pair_count * ((end_count + pair_count - 1) // pair_count)
    hid = weight_in.shape[1]
    feat = weight_in.shape[0]
    far, near = gather_features(node_features)
    place = jnp.stack([lax.axis_index("pair"), lax.axis_index("state") % 2]).astype(jnp.int32)
    atoms_here = node_features.shape[0]
    own_orbitals = lax.dynamic_slice_in_dim(atom_orbitals, place[0] * atoms_here, atoms_here)
    valid = (jnp.arange(ORB)[None, :] < own_orbitals[:, None]).astype(jnp.float32)
    valid = valid.reshape(1, atoms_here * ORB)
    onsite_row = onsite.reshape(1, -1)
    smem = pl.BlockSpec(memory_space=pltpu.SMEM)
    vmem = pl.BlockSpec(memory_space=pltpu.VMEM)
    hbm = pl.BlockSpec(memory_space=pl.ANY)
    groups = block_count + (2 * block_count + state_rows - 1) // state_rows
    limit = pltpu.CompilerParams(vmem_limit_bytes=VMEM_LIMIT)
    payload, own_split = pl.pallas_call(
        functools.partial(prepare_kernel, block_count),
        out_shape=[
            jax.ShapeDtypeStruct((groups * state_rows, WIDE), jnp.bfloat16),
            jax.ShapeDtypeStruct((block_count, 2 * state_rows, ROWS), jnp.bfloat16),
        ],
        in_specs=[vmem, vmem, vmem],
        out_specs=[vmem, vmem],
        scratch_shapes=[pltpu.VMEM((groups * state_rows, BO), jnp.bfloat16)],
        compiler_params=limit,
        name="prepare",
    )(states_in, onsite_row, valid)
    payload = after(payload, *[far[offset] for offset in sorted(far)[1:]])
    pieces, places, bundle = spread_features(far, near)
    pair_blocks, weight_in, weight_out = after(
        (pair_blocks, weight_in, weight_out), far[max(far)]
    )
    pieces = [piece.reshape(-1, ATOM_BLK, piece.shape[1]) for piece in pieces]
    places = [
        (start // ATOM_BLK, rows // ATOM_BLK, first // ATOM_BLK, column)
        for start, rows, first, column in places
    ]
    cube = weight_out.reshape(hid, ORB, ORB).astype(jnp.float32)
    pad = ((0, 0), (0, PAD_ORB - ORB), (0, 0))
    weights = jnp.stack(
        [
            jnp.pad(cube.transpose(2, 1, 0), pad).reshape(ORB * PAD_ORB, hid),
            jnp.pad(cube.transpose(1, 2, 0), pad).reshape(ORB * PAD_ORB, hid),
        ]
    ).astype(jnp.bfloat16)

    tables = pl.pallas_call(
        functools.partial(tables_kernel, pair_count, block_count),
        out_shape=jax.ShapeDtypeStruct((8, 2 * pairs), jnp.int32),
        in_specs=[smem, vmem, vmem],
        out_specs=vmem,
        compiler_params=limit,
        name="tables",
    )(place, pair_blocks, pair_live.reshape(1, pairs))
    state_index = lax.axis_index("state")
    quarter = node_features.shape[1]
    parts = weight_in.reshape(feat // quarter, quarter, hid)
    order = state_index ^ jnp.arange(feat // quarter)
    weights_here = jnp.take(parts, order, axis=0).reshape(feat, hid)
    other_split = swap(own_split, "state", 1)
    own_fields, spots = gather_fields(
        payload.reshape(groups, state_rows, WIDE), (tables, weights_here, weights, other_split)
    )
    fields = []
    for entry in own_fields:
        fields += [entry, swap(entry, "state", 1)]
    kept, sent = run_filter(
        places, spots, blocks, slots, tables, own_split, other_split, weights_here,
        bias_in.reshape(1, hid), weights, pieces, fields,
    )
    got = swap(sent, "state", 1).astype(jnp.float32)
    first = states_in * onsite_row + (kept[0] + got[0]) * valid
    again = (kept[1] + got[1]) * valid
    return first, 2.0 * (first * onsite_row + again) - states_in


def solution(mesh):
    return jax.shard_map(
        per_device,
        mesh=mesh,
        in_specs=(P("state", "pair"), P("pair"), P("pair", "state"), P(), P(), P(), P(), P(), P()),
        out_specs=(P("state", "pair"), P("state", "pair")),
        check_vma=False,
    )
```
